128 devices in a mesh: row: 16 (over y_hi, x, core), col: 8 (over y_lo, z).
Axes of the slice: x: 4, y: 4 (y_hi: 2, y_lo: 2; y = y_hi * 2 + y_lo), z: 4, core: 2. Of those that a mesh axis runs over, the one named last changes fastest.
Arguments:
- stem: float32 [2, 16, 8, 4, 256, 256], P(None, 'row', 'col'), may hold values from -6 to 6
- branch_one: float32 [2, 256, 256], replicated, may hold values from -0.25 to 0.25
- branch_two: float32 [2, 256, 256], replicated, may hold values from -0.25 to 0.25
- branch_three: float32 [2, 256, 256], replicated, may hold values from -0.25 to 0.25
- branch_four: float32 [2, 256, 256], replicated, may hold values from -0.25 to 0.25
- relabel: int32 [256], replicated, may hold values from 0 to 255, each once
Outputs:
- amplitudes: float32 [2, 8, 256, 256], P(None, None, 'col', 'row')
The draws below stay inside these ranges and needn't reach their ends.
Inputs may be any that keep to these rules, and one draw needn't show every extreme that they name: `relabel`: each of the 256 values appears once.
All inputs are finite; a program needn't handle non-finite values.
Results may differ from the reference program's by a relative error of at most 0.00007.
Values sent between devices are 32-bit elements; how exact they have to be, the bound alone decides.
A program may use at most 128 MiB of HBM per device.

```python
import jax
import jax.numpy as jnp
from jax import lax

GROUP = 256
FOLD = 4
N_ROW = 16
N_COL = 8


def block_scale(rng, extent, cuts, smallest, high):
    factor_of = 1.0
    for axis_at, parts in cuts:
        draws = jax.random.uniform(jax.random.fold_in(jax.random.fold_in(rng, 6), axis_at), (parts,), jnp.float32, smallest / len(cuts), high / len(cuts))
        factor_of = factor_of * jnp.repeat(jnp.exp(draws), extent[axis_at] // parts).reshape((-1,) + (1,) * (len(extent) - 1 - axis_at))
    return factor_of


def bell_draw(own_key, shape, width, limit, pieces=(), dtype=jnp.bfloat16):
    gain = block_scale(own_key, shape, pieces, -0.22, 0.18) if pieces else 1.0
    drawn = jax.random.normal(own_key, shape, jnp.float32) * width * gain
    return jnp.minimum(jnp.maximum(drawn, -limit), limit).astype(dtype)


def setup_inputs(seed: int = 0) -> dict:
    key_list = jax.random.split(jax.random.key(seed), 7)
    return {
        "stem": bell_draw(key_list[0], (2, N_ROW, N_COL, FOLD, GROUP, GROUP), 1.0, 6.0, ((1, 16), (2, 8)), jnp.float32),
        "branch_one": bell_draw(key_list[1], (2, GROUP, GROUP), (2 * GROUP) ** -0.5, 0.25, (), jnp.float32),
        "branch_two": bell_draw(key_list[2], (2, GROUP, GROUP), (2 * GROUP) ** -0.5, 0.25, (), jnp.float32),
        "branch_three": bell_draw(key_list[3], (2, GROUP, GROUP), (2 * GROUP) ** -0.5, 0.25, (), jnp.float32),
        "branch_four": bell_draw(key_list[4], (2, GROUP, GROUP), (2 * GROUP) ** -0.5, 0.25, (), jnp.float32),
        "relabel": jax.random.permutation(key_list[5], GROUP).astype(jnp.int32),
    }


def absorb(pattern, matrix, stem_field):
    highest = lax.Precision.HIGHEST
    real_part = jnp.einsum(pattern, matrix[0], stem_field[0], precision=highest) - jnp.einsum(pattern, matrix[1], stem_field[1], precision=highest)
    imag_part = jnp.einsum(pattern, matrix[0], stem_field[1], precision=highest) + jnp.einsum(pattern, matrix[1], stem_field[0], precision=highest)
    return jnp.stack([real_part, imag_part])


def reference(stem, branch_one, branch_two, branch_three, branch_four, relabel):
    row_count = N_ROW
    col_count = N_COL
    stem_field = absorb("pu,abfuv->abfpv", branch_one, stem)
    stem_field = stem_field[..., relabel]
    stem_field = absorb("qv,abfuv->abfuq", branch_two, stem_field)
    stem_field = stem_field.reshape(2, row_count, col_count, FOLD, col_count, GROUP // col_count, row_count, GROUP // row_count)
    matrix_three = branch_three.reshape(2, row_count, GROUP // row_count, row_count, GROUP // row_count)
    matrix_four = branch_four.reshape(2, col_count, GROUP // col_count, col_count, GROUP // col_count)
    stem_field = absorb("xyah,abfkilh->xbfkily", matrix_three, stem_field)
    stem_field = absorb("xybi,abfkilh->axfkylh", matrix_four, stem_field)
    summed = jnp.sum(stem_field, axis=(1, 3))
    factor = (FOLD * row_count) ** -0.5
    return summed.reshape(2, col_count, GROUP, GROUP) * factor
```

```python
import functools

import jax
import jax.numpy as jnp
from jax import lax
from jax.experimental import pallas as pl
from jax.experimental.pallas import tpu as pltpu
from jax.sharding import PartitionSpec as P

MESH = pl.DeviceIdType.MESH
F32, BF16 = jnp.float32, jnp.bfloat16
NT = (((1,), (1,)), ((), ()))
NN = (((1,), (0,)), ((), ()))

OFFSETS = ((1, 2), (1, 1), (1, 3), (0, 2), (1, 0), (0, 1), (0, 3), (0, 0))
PIECES = 4


def dot(lhs, rhs, dims):
    return lax.dot_general(lhs, rhs, dims, preferred_element_type=F32)


def split(value):
    high = value.astype(BF16)
    return high, (value - high.astype(F32)).astype(BF16)


def hops(offset):
    return offset[0] + min(offset[1], 4 - offset[1])


def shifted(index, offset, sign):
    high, low = index // 4, index % 4
    return ((high + 2 + sign * offset[0]) % 2) * 4 + (low + 4 + sign * offset[1]) % 4


def lanes_to(value, source, target):
    amount = (target - source) * 32 % 128
    return value if amount == 0 else pltpu.roll(value, amount, value.ndim - 1)


def regroup(tiles, lane_group):
    out = []
    for j in range(4):
        made = lanes_to(tiles[0], j, 0)
        for i in range(1, 4):
            made = jnp.where(lane_group == i, lanes_to(tiles[i], j, i), made)
        out.append(made)
    return out


def put_complex(ref, real_part, imag_part, rows, width, base=0):
    for part, (re, im) in enumerate(zip(split(real_part), split(imag_part))):
        at = base + part * 2 * rows
        ref[at : at + rows, 0:width] = re
        ref[at : at + rows, width : 2 * width] = -im
        ref[at + rows : at + 2 * rows, 0:width] = im
        ref[at + rows : at + 2 * rows, width : 2 * width] = re


def kernel(
    factor, stem, one, two, three, four, relabel, out,
    stem_v, one_v, two_v, three_v, four_v, relabel_v,
    k_l, m_h, m_l, m_lhs, t_h, t_l, o_h, o_l, y_lhs, f_h, f_l,
    w_out, w_in, packed, landed, sums,
    stem_sem, one_sem, two_sem, three_sem, four_sem, relabel_sem,
    core_send, core_recv, far_send, far_recv,
):
    row, col = lax.axis_index("row"), lax.axis_index("col")
    chip, core = row // 2, row % 2
    row_to = [shifted(chip, o, 1) for o in OFFSETS]
    col_to = [shifted(col, o, 1) for o in OFFSETS]
    col_from = [shifted(col, o, -1) for o in OFFSETS]
    order = sorted(
        ((j, k) for j in range(8) for k in range(8) if (j, k) != (7, 7)),
        key=lambda jk: -hops(OFFSETS[jk[0]]) - hops(OFFSETS[jk[1]]),
    )

    pltpu.make_async_copy(relabel, relabel_v, relabel_sem).start()
    column = pl.multiple_of(row // 8 * 128, 128)
    pltpu.make_async_copy(three.at[:, :, :, pl.ds(column, 128)], three_v, three_sem).start()
    for j in range(8):
        for half in range(2):
            source = 1 - core if half == 0 else core
            pltpu.make_async_copy(two.at[:, row_to[j], source], two_v.at[half, :, j], two_sem).start()
    for c in range(2):
        for f in range(4):
            pltpu.make_async_copy(stem.at[c, f], stem_v.at[c, f], stem_sem.at[c]).start()
    for k in range(8):
        pltpu.make_async_copy(one.at[:, col_to[k]], one_v.at[:, k], one_sem).start()
    pltpu.make_async_copy(four, four_v, four_sem).start()

    barrier = pltpu.get_barrier_semaphore()
    for j, k in order:
        pl.semaphore_signal(barrier, inc=1, device_id=(row_to[j] * 2 + core, col_to[k]), device_id_type=MESH)
    pl.semaphore_signal(barrier, inc=1, device_id=(chip * 2 + 1 - core, col), device_id_type=MESH)

    pltpu.make_async_copy(three_v, three_v, three_sem).wait()
    lane = lax.broadcasted_iota(jnp.int32, (16, 128), 1)
    turned = (128 - row % 8 * 16) % 128
    diagonal = (
        lax.broadcasted_iota(jnp.int32, (128, 128), 0) // 16 == lax.broadcasted_iota(jnp.int32, (128, 128), 1) // 16
    )
    block = []
    for c in range(2):
        piece = three_v[c, 0]
        for x in range(1, 16):
            piece = piece + three_v[c, x]
        piece = jnp.where(lane < 16, pltpu.roll(piece * factor, turned, 1), 0.0)
        for amount in (16, 32, 64):
            piece = piece + pltpu.roll(piece, amount, 1)
        block.append(jnp.where(diagonal, jnp.concatenate([piece] * 8, axis=0), 0.0))
    put_complex(k_l, block[0], block[1], 128, 128)

    pltpu.make_async_copy(relabel_v, relabel_v, relabel_sem).wait()
    names = jnp.broadcast_to(relabel_v[...].reshape(1, 256), (256, 256))
    pick = jnp.where(lax.broadcasted_iota(jnp.int32, (256, 256), 0) == names, 1.0, 0.0).astype(BF16)
    pltpu.make_async_copy(two_v, two_v, two_sem).wait()
    for half in range(2):
        pair = two_v[half].reshape(256, 256)
        for ref, part in zip((m_h, m_l), split(pair)):
            ref[:, half * 256 : half * 256 + 256] = dot(part, pick, NT).astype(BF16)
    both = dot(k_l[...], m_h[...], NN)
    m_all = both[0:256] + both[256:512] + dot(k_l[0:256], m_l[...], NN)
    for half in range(2):
        at = half * 256
        put_complex(m_lhs, m_all[0:128, at : at + 256], m_all[128:256, at : at + 256], 128, 256, half * 512)

    for c in range(2):
        pltpu.make_async_copy(stem_v.at[c], stem_v.at[c], stem_sem.at[c]).wait()
        total = (stem_v[c, 0] + stem_v[c, 1]) + (stem_v[c, 2] + stem_v[c, 3])
        t_h[:, c * 256 : c * 256 + 256], t_l[:, c * 256 : c * 256 + 256] = split(total)
    pltpu.make_async_copy(one_v, one_v, one_sem).wait()
    for c in range(2):
        o_h[:, c * 256 : c * 256 + 256], o_l[:, c * 256 : c * 256 + 256] = split(one_v[c].reshape(256, 256))

    def absorbed(half):
        base = half * 512
        first = dot(m_lhs[base : base + 512], t_h[...], NT)
        y = first[0:256] + first[256:512] + dot(m_lhs[base : base + 256], t_l[...], NT)
        put_complex(y_lhs, y[0:128], y[128:256], 128, 256, base)
        second = dot(y_lhs[base : base + 512], o_h[...], NT)
        return second[0:256] + second[256:512] + dot(y_lhs[base : base + 256], o_l[...], NT)

    rows = 128 // PIECES
    w_out[...] = absorbed(0).reshape(2, 128, 256)
    pl.semaphore_wait(barrier, 64)

    def core_copy(p):
        return pltpu.make_async_remote_copy(
            src_ref=w_out.at[:, p * rows : (p + 1) * rows],
            dst_ref=w_in.at[:, p * rows : (p + 1) * rows],
            send_sem=core_send.at[p],
            recv_sem=core_recv.at[p],
            device_id=(chip * 2 + 1 - core, col),
            device_id_type=MESH,
        )

    for p in range(PIECES):
        core_copy(p).start()
    mine = absorbed(1).reshape(2, 128, 256)

    chips = 8 // PIECES
    groups = lax.broadcasted_iota(jnp.int32, (chips, 8, 128), 2) // 32
    for p in range(PIECES):
        core_copy(p).wait_recv()
        added = mine[:, p * rows : (p + 1) * rows] + w_in[:, p * rows : (p + 1) * rows]
        added = added.reshape(2, chips, 2, 8, 256)
        for h in range(2):
            tiles = [added[g // 2, :, g % 2, :, h * 128 : h * 128 + 128] for g in range(4)]
            for q, made in enumerate(regroup(tiles, groups)):
                packed[p * chips : (p + 1) * chips, h * 4 + q] = made
        for j, k in order:
            if j // chips == p:
                pltpu.make_async_remote_copy(
                    src_ref=packed.at[j, k],
                    dst_ref=landed.at[j * 8 + k],
                    send_sem=far_send,
                    recv_sem=far_recv,
                    device_id=(row_to[j] * 2 + core, col_to[k]),
                    device_id_type=MESH,
                ).start()

    pltpu.make_async_copy(four_v, four_v, four_sem).wait()
    for c in range(2):
        f_h[c * 256 : c * 256 + 256], f_l[c * 256 : c * 256 + 256] = split(four_v[c])

    pltpu.make_async_copy(landed.at[0:63], landed.at[0:63], far_recv).wait()
    for k in range(8):
        total = landed[k]
        for j in range(1, 7):
            total = total + landed[j * 8 + k]
        total = total + (landed[56 + k] if k < 7 else packed[7, 7])
        sums[col_from[k]] = total
    group = lax.broadcasted_iota(jnp.int32, (8, 128), 1) // 32
    v = jnp.concatenate(
        [jnp.concatenate(regroup([sums[h * 4 + q] for q in range(4)], group), axis=0) for h in range(2)], axis=1
    )
    v_h, v_l = split(v)
    first = dot(jnp.concatenate([v_h, v_l], axis=0), f_h[...], NT)
    made = first[0:32] + first[32:64] + dot(v_h, f_l[...], NT)
    result = (made[0:16, 0:256] - made[16:32, 256:512], made[0:16, 256:512] + made[16:32, 0:256])
    for c in range(2):
        for b in range(8):
            out[c, b] = result[c][:, b * 32 : b * 32 + 32]

    for p in range(PIECES):
        core_copy(p).wait_send()
    pltpu.make_async_copy(landed.at[0:63], landed.at[0:63], far_send).wait()


def body(stem, branch_one, branch_two, branch_three, branch_four, relabel):
    factor = (stem.shape[3] * lax.axis_size("row")) ** (-0.5)
    any_space = pl.BlockSpec(memory_space=pltpu.HBM)
    dma = pltpu.SemaphoreType.DMA
    made = pl.pallas_call(
        functools.partial(kernel, factor),
        out_shape=jax.ShapeDtypeStruct((2, 8, 16, 32), F32),
        in_specs=[any_space] * 6,
        out_specs=pl.BlockSpec(memory_space=pltpu.VMEM),
        scratch_shapes=[
            pltpu.VMEM((2, 4, 256, 256), F32),
            pltpu.VMEM((2, 8, 32, 256), F32),
            pltpu.VMEM((2, 2, 8, 16, 256), F32),
            pltpu.VMEM((2, 16, 16, 128), F32),
            pltpu.VMEM((2, 256, 256), F32),
            pltpu.VMEM((256,), jnp.int32),
            pltpu.VMEM((512, 256), BF16),
            pltpu.VMEM((256, 512), BF16),
            pltpu.VMEM((256, 512), BF16),
            pltpu.VMEM((1024, 512), BF16),
            pltpu.VMEM((256, 512), BF16),
            pltpu.VMEM((256, 512), BF16),
            pltpu.VMEM((256, 512), BF16),
            pltpu.VMEM((256, 512), BF16),
            pltpu.VMEM((1024, 512), BF16),
            pltpu.VMEM((512, 256), BF16),
            pltpu.VMEM((512, 256), BF16),
            pltpu.VMEM((2, 128, 256), F32),
            pltpu.VMEM((2, 128, 256), F32),
            pltpu.VMEM((8, 8, 8, 128), F32),
            pltpu.VMEM((64, 8, 128), F32),
            pltpu.VMEM((8, 8, 128), F32),
            dma((2,)), dma, dma, dma, dma, dma,
            dma((PIECES,)), dma((PIECES,)), dma, dma,
        ],
        compiler_params=pltpu.CompilerParams(
            collective_id=0, has_side_effects=True, vmem_limit_bytes=62 << 20
        ),
        name="contract",
    )(
        stem.reshape(2, 4, 256, 256),
        branch_one.reshape(2, 8, 32, 256),
        branch_two.reshape(2, 8, 2, 16, 256),
        branch_three.reshape(2, 16, 16, 256),
        branch_four,
        relabel,
    )
    return made.transpose(0, 1, 3, 2)


def solution(mesh):
    in_specs = (P(None, "row", "col", None, None, None), P(), P(), P(), P(), P())
    out_specs = P(None, None, "col", "row")
    return jax.shard_map(body, mesh=mesh, in_specs=in_specs, out_specs=out_specs, check_vma=False)
```

```python
import functools

import jax
import jax.numpy as jnp
from jax import lax
from jax.experimental import pallas as pl
from jax.experimental.pallas import tpu as pltpu
from jax.sharding import PartitionSpec as P

MESH = pl.DeviceIdType.MESH
F32, BF16 = jnp.float32, jnp.bfloat16
NT = (((1,), (1,)), ((), ()))
NN = (((1,), (0,)), ((), ()))

OFFSETS = ((1, 2), (1, 1), (1, 3), (0, 2), (1, 0), (0, 1), (0, 3), (0, 0))
PIECES = 4


def dot(lhs, rhs, dims):
    return lax.dot_general(lhs, rhs, dims, preferred_element_type=F32)


def split(value):
    high = value.astype(BF16)
    return high, (value - high.astype(F32)).astype(BF16)


def hops(offset):
    return offset[0] + min(offset[1], 4 - offset[1])


def shifted(index, offset, sign):
    high, low = index // 4, index % 4
    return ((high + 2 + sign * offset[0]) % 2) * 4 + (low + 4 + sign * offset[1]) % 4


def lanes_to(value, source, target):
    amount = (target - source) * 32 % 128
    return value if amount == 0 else pltpu.roll(value, amount, value.ndim - 1)


def regroup(tiles, lane_group):
    out = []
    for j in range(4):
        made = lanes_to(tiles[0], j, 0)
        for i in range(1, 4):
            made = jnp.where(lane_group == i, lanes_to(tiles[i], j, i), made)
        out.append(made)
    return out


def put_left(ref, real_part, imag_part, rows, width, row=0, column=0):
    parts = list(zip(split(real_part), split(imag_part)))
    for block, (re, im) in enumerate((parts[0], parts[1], parts[0])):
        at = column + block * 2 * width
        ref[row : row + rows, at : at + width] = re
        ref[row : row + rows, at + width : at + 2 * width] = -im
        ref[row + rows : row + 2 * rows, at : at + width] = im
        ref[row + rows : row + 2 * rows, at + width : at + 2 * width] = re


def kernel(
    factor, stem, one, two, three, four, relabel, out,
    stem_v, one_v, two_v, three_v, four_v, relabel_v,
    k_lhs, m_rhs, m_lhs, t_rhs, o_lhs, s_rhs, f_h, f_l,
    w_out, w_in, packed, landed, sums,
    stem_sem, one_sem, two_sem, three_sem, four_sem, relabel_sem,
    core_send, core_recv, far_send, far_recv, met, all_met,
):
    row, col = lax.axis_index("row"), lax.axis_index("col")
    chip, core = row // 2, row % 2
    partner = (chip * 2 + 1 - core, col)
    row_to = [shifted(chip, o, 1) for o in OFFSETS]
    col_to = [shifted(col, o, 1) for o in OFFSETS]
    col_from = [shifted(col, o, -1) for o in OFFSETS]
    order = sorted(
        ((j, k) for j in range(8) for k in range(8) if (j, k) != (7, 7)),
        key=lambda jk: -hops(OFFSETS[jk[0]]) - hops(OFFSETS[jk[1]]),
    )

    pltpu.make_async_copy(relabel, relabel_v, relabel_sem).start()
    column = pl.multiple_of(row // 8 * 128, 128)
    pltpu.make_async_copy(three.at[:, :, :, pl.ds(column, 128)], three_v, three_sem).start()
    for j in range(8):
        for half in range(2):
            source = 1 - core if half == 0 else core
            pltpu.make_async_copy(two.at[:, row_to[j], source], two_v.at[half, :, j], two_sem).start()
    for k in range(8):
        pltpu.make_async_copy(one.at[:, col_to[k]], one_v.at[:, k], one_sem).start()
    for u in range(2):
        for c in range(2):
            for f in range(4):
                pltpu.make_async_copy(
                    stem.at[c, f, u * 128 : u * 128 + 128], stem_v.at[u, c, f], stem_sem.at[u]
                ).start()

    barrier = pltpu.get_barrier_semaphore()

    @pl.when(core == 1)
    def _():
        pl.semaphore_signal(barrier, inc=1, device_id=partner, device_id_type=MESH)

    @pl.when(core == 0)
    def _():
        pl.semaphore_wait(barrier, 1)
        pl.semaphore_signal(met, inc=1, device_id=partner, device_id_type=MESH)

    @pl.when(core == 1)
    def _():
        pl.semaphore_wait(met, 1)
        for j, k in order:
            pl.semaphore_signal(barrier, inc=1, device_id=(row_to[j] * 2 + 1, col_to[k]), device_id_type=MESH)

    pltpu.make_async_copy(three_v, three_v, three_sem).wait()
    lane = lax.broadcasted_iota(jnp.int32, (16, 128), 1)
    turned = (128 - row % 8 * 16) % 128
    diagonal = (
        lax.broadcasted_iota(jnp.int32, (128, 128), 0) // 16 == lax.broadcasted_iota(jnp.int32, (128, 128), 1) // 16
    )
    block = []
    for c in range(2):
        piece = three_v[c, 0]
        for x in range(1, 16):
            piece = piece + three_v[c, x]
        piece = jnp.where(lane < 16, pltpu.roll(piece * factor, turned, 1), 0.0)
        for amount in (16, 32, 64):
            piece = piece + pltpu.roll(piece, amount, 1)
        block.append(jnp.where(diagonal, jnp.concatenate([piece] * 8, axis=0), 0.0))
    put_left(k_lhs, block[0], block[1], 128, 128)

    pltpu.make_async_copy(relabel_v, relabel_v, relabel_sem).wait()
    names = jnp.broadcast_to(relabel_v[...].reshape(1, 256), (256, 256))
    pick = jnp.where(lax.broadcasted_iota(jnp.int32, (256, 256), 0) == names, 1.0, 0.0).astype(BF16)
    pltpu.make_async_copy(two_v, two_v, two_sem).wait()
    for half in range(2):
        high, low = (dot(part, pick, NT).astype(BF16) for part in split(two_v[half].reshape(256, 256)))
        for block_at, part in enumerate((high, high, low)):
            m_rhs[block_at * 256 : block_at * 256 + 256, half * 256 : half * 256 + 256] = part
    m_all = dot(k_lhs[...], m_rhs[...], NN)
    for half in range(2):
        at = half * 256
        put_left(m_lhs, m_all[0:128, at : at + 256], m_all[128:256, at : at + 256], 128, 256, half * 256)

    pltpu.make_async_copy(one_v, one_v, one_sem).wait()
    for u in range(2):
        re, im = (one_v[c].reshape(256, 256)[:, u * 128 : u * 128 + 128] for c in range(2))
        put_left(o_lhs, re, im, 256, 128, 0, u * 768)
    first = None
    for u in range(2):
        pltpu.make_async_copy(stem_v.at[u], stem_v.at[u], stem_sem.at[u]).wait()
        for c in range(2):
            high, low = split((stem_v[u, c, 0] + stem_v[u, c, 1]) + (stem_v[u, c, 2] + stem_v[u, c, 3]))
            for block_at, part in enumerate((high, high, low)):
                at = u * 768 + block_at * 256 + c * 128
                t_rhs[at : at + 128] = part
        part = dot(o_lhs[:, u * 768 : u * 768 + 768], t_rhs[u * 768 : u * 768 + 768], NN)
        first = part if first is None else first + part
    for c in range(2):
        high, low = split(first[c * 256 : c * 256 + 256])
        for block_at, part in enumerate((high, high, low)):
            at = block_at * 512 + c * 256
            s_rhs[:, at : at + 256] = part
    pltpu.make_async_copy(four, four_v, four_sem).start()

    rows = 128 // PIECES
    w_out[...] = dot(m_lhs[0:256], s_rhs[...], NT).reshape(2, 128, 256)

    def core_copy(p):
        return pltpu.make_async_remote_copy(
            src_ref=w_out.at[:, p * rows : (p + 1) * rows],
            dst_ref=w_in.at[:, p * rows : (p + 1) * rows],
            send_sem=core_send.at[p],
            recv_sem=core_recv.at[p],
            device_id=partner,
            device_id_type=MESH,
        )

    for p in range(PIECES):
        core_copy(p).start()
    mine = dot(m_lhs[256:512], s_rhs[...], NT).reshape(2, 128, 256)

    @pl.when(core == 1)
    def _():
        pl.semaphore_wait(barrier, 63)
        pl.semaphore_signal(all_met, inc=1, device_id=partner, device_id_type=MESH)

    @pl.when(core == 0)
    def _():
        pl.semaphore_wait(all_met, 1)

    chips = 8 // PIECES
    groups = lax.broadcasted_iota(jnp.int32, (chips, 8, 128), 2) // 32
    for p in range(PIECES):
        core_copy(p).wait_recv()
        added = mine[:, p * rows : (p + 1) * rows] + w_in[:, p * rows : (p + 1) * rows]
        added = added.reshape(2, chips, 2, 8, 256)
        for h in range(2):
            tiles = [added[g // 2, :, g % 2, :, h * 128 : h * 128 + 128] for g in range(4)]
            for q, made in enumerate(regroup(tiles, groups)):
                packed[p * chips : (p + 1) * chips, h * 4 + q] = made
        for j, k in order:
            if j // chips == p:
                pltpu.make_async_remote_copy(
                    src_ref=packed.at[j, k],
                    dst_ref=landed.at[j * 8 + k],
                    send_sem=far_send,
                    recv_sem=far_recv,
                    device_id=(row_to[j] * 2 + core, col_to[k]),
                    device_id_type=MESH,
                ).start()

    pltpu.make_async_copy(four_v, four_v, four_sem).wait()
    for c in range(2):
        f_h[c * 256 : c * 256 + 256], f_l[c * 256 : c * 256 + 256] = split(four_v[c])

    pltpu.make_async_copy(landed.at[0:63], landed.at[0:63], far_recv).wait()
    for k in range(8):
        total = landed[k]
        for j in range(1, 7):
            total = total + landed[j * 8 + k]
        total = total + (landed[56 + k] if k < 7 else packed[7, 7])
        sums[col_from[k]] = total
    group = lax.broadcasted_iota(jnp.int32, (8, 128), 1) // 32
    v = jnp.concatenate(
        [jnp.concatenate(regroup([sums[h * 4 + q] for q in range(4)], group), axis=0) for h in range(2)], axis=1
    )
    v_h, v_l = split(v)
    first = dot(jnp.concatenate([v_h, v_l], axis=0), f_h[...], NT)
    made = first[0:32] + first[32:64] + dot(v_h, f_l[...], NT)
    result = (made[0:16, 0:256] - made[16:32, 256:512], made[0:16, 256:512] + made[16:32, 0:256])
    for c in range(2):
        for b in range(8):
            out[c, b] = result[c][:, b * 32 : b * 32 + 32]

    for p in range(PIECES):
        core_copy(p).wait_send()
    pltpu.make_async_copy(landed.at[0:63], landed.at[0:63], far_send).wait()


def body(stem, branch_one, branch_two, branch_three, branch_four, relabel):
    factor = (stem.shape[3] * lax.axis_size("row")) ** (-0.5)
    any_space = pl.BlockSpec(memory_space=pltpu.HBM)
    dma = pltpu.SemaphoreType.DMA
    made = pl.pallas_call(
        functools.partial(kernel, factor),
        out_shape=pltpu.VMEM((2, 8, 16, 32), F32),
        in_specs=[any_space] * 6,
        out_specs=pl.BlockSpec(memory_space=pltpu.VMEM),
        scratch_shapes=[
            pltpu.VMEM((2, 2, 4, 128, 256), F32),
            pltpu.VMEM((2, 8, 32, 256), F32),
            pltpu.VMEM((2, 2, 8, 16, 256), F32),
            pltpu.VMEM((2, 16, 16, 128), F32),
            pltpu.VMEM((2, 256, 256), F32),
            pltpu.VMEM((256,), jnp.int32),
            pltpu.VMEM((256, 768), BF16),
            pltpu.VMEM((768, 512), BF16),
            pltpu.VMEM((512, 1536), BF16),
            pltpu.VMEM((1536, 256), BF16),
            pltpu.VMEM((512, 1536), BF16),
            pltpu.VMEM((256, 1536), BF16),
            pltpu.VMEM((512, 256), BF16),
            pltpu.VMEM((512, 256), BF16),
            pltpu.VMEM((2, 128, 256), F32),
            pltpu.VMEM((2, 128, 256), F32),
            pltpu.VMEM((8, 8, 8, 128), F32),
            pltpu.VMEM((64, 8, 128), F32),
            pltpu.VMEM((8, 8, 128), F32),
            dma((2,)), dma, dma, dma, dma, dma,
            dma((PIECES,)), dma((PIECES,)), dma, dma,
            pltpu.SemaphoreType.REGULAR, pltpu.SemaphoreType.REGULAR,
        ],
        compiler_params=pltpu.CompilerParams(
            collective_id=0, has_side_effects=True, vmem_limit_bytes=40 << 20
        ),
        name="contract",
    )(
        *(
            pltpu.with_memory_space_constraint(value, pltpu.HBM)
            for value in (
                stem.reshape(2, 4, 256, 256),
                branch_one.reshape(2, 8, 32, 256),
                branch_two.reshape(2, 8, 2, 16, 256),
                branch_three.reshape(2, 16, 16, 256),
                branch_four,
                relabel,
            )
        )
    )
    return made.transpose(0, 1, 3, 2)


def solution(mesh):
    in_specs = (P(None, "row", "col", None, None, None), P(), P(), P(), P(), P())
    out_specs = P(None, None, "col", "row")
    return jax.shard_map(body, mesh=mesh, in_specs=in_specs, out_specs=out_specs, check_vma=False)
```

```python
import functools

import jax
import jax.numpy as jnp
from jax import lax
from jax.experimental import pallas as pl
from jax.experimental.pallas import tpu as pltpu
from jax.sharding import PartitionSpec as P

MESH = pl.DeviceIdType.MESH
F32, BF16 = jnp.float32, jnp.bfloat16
NT = (((1,), (1,)), ((), ()))
NN = (((1,), (0,)), ((), ()))

OFFSETS = ((1, 2), (1, 1), (1, 3), (0, 2), (1, 0), (0, 1), (0, 3), (0, 0))
PIECES = 4


def dot(lhs, rhs, dims):
    return lax.dot_general(lhs, rhs, dims, preferred_element_type=F32)


def split(value):
    high = value.astype(BF16)
    return high, (value - high.astype(F32)).astype(BF16)


def hops(offset):
    return offset[0] + min(offset[1], 4 - offset[1])


def shifted(index, offset, sign):
    high, low = index // 4, index % 4
    return ((high + 2 + sign * offset[0]) % 2) * 4 + (low + 4 + sign * offset[1]) % 4


def lanes_to(value, source, target):
    amount = (target - source) * 32 % 128
    return value if amount == 0 else pltpu.roll(value, amount, value.ndim - 1)


def regroup(tiles, lane_group):
    out = []
    for j in range(4):
        made = lanes_to(tiles[0], j, 0)
        for i in range(1, 4):
            made = jnp.where(lane_group == i, lanes_to(tiles[i], j, i), made)
        out.append(made)
    return out


def put_left(ref, real_part, imag_part, rows, width, row=0, column=0):
    for block, (re, im) in enumerate(zip(split(real_part), split(imag_part))):
        at = column + block * 2 * width
        ref[row : row + rows, at : at + width] = re
        ref[row : row + rows, at + width : at + 2 * width] = -im
        ref[row + rows : row + 2 * rows, at : at + width] = im
        ref[row + rows : row + 2 * rows, at + width : at + 2 * width] = re


def three_dots(left_high, left_low, right_high, right_low, dims):
    return dot(left_high, right_high, dims) + dot(left_low, right_high, dims) + dot(left_high, right_low, dims)


def put_three(ref, real_part, imag_part):
    for i, value in enumerate((real_part, imag_part, real_part + imag_part)):
        for part, made in enumerate(split(value)):
            ref[i, part] = made


def product(left, right, dims):
    rr, ii, ss = (three_dots(left[i, 0], left[i, 1], right[i, 0], right[i, 1], dims) for i in range(3))
    return rr - ii, ss - rr - ii


def kernel(
    factor, stem, one, two, three, four, relabel, out,
    stem_v, one_v, two_v, three_v, four_v, relabel_v,
    k_lhs, m_rhs, m_lhs, t_rhs, o_lhs, s_rhs, f_h, f_l,
    w_out, w_in, packed, landed, sums,
    stem_sem, one_sem, two_sem, three_sem, four_sem, relabel_sem,
    core_send, core_recv, far_send, far_recv, met, all_met,
):
    row, col = lax.axis_index("row"), lax.axis_index("col")
    chip, core = row // 2, row % 2
    partner = (chip * 2 + 1 - core, col)
    row_to = [shifted(chip, o, 1) for o in OFFSETS]
    col_to = [shifted(col, o, 1) for o in OFFSETS]
    col_from = [shifted(col, o, -1) for o in OFFSETS]
    order = sorted(
        ((j, k) for j in range(8) for k in range(8) if (j, k) != (7, 7)),
        key=lambda jk: -hops(OFFSETS[jk[0]]) - hops(OFFSETS[jk[1]]),
    )

    pltpu.make_async_copy(relabel, relabel_v, relabel_sem).start()
    column = pl.multiple_of(row // 8 * 128, 128)
    for x in range(16):
        pltpu.make_async_copy(three.at[:, x, :, pl.ds(column, 128)], three_v.at[:, x], three_sem).start()
    for j in range(8):
        for half in range(2):
            source = 1 - core if half == 0 else core
            pltpu.make_async_copy(two.at[:, row_to[j], source], two_v.at[half, :, j], two_sem).start()
    for k in range(8):
        pltpu.make_async_copy(one.at[:, col_to[k]], one_v.at[:, k], one_sem).start()
    for c in range(2):
        for f in range(0, 4, 2):
            pltpu.make_async_copy(stem.at[c, f : f + 2], stem_v.at[c, f : f + 2], stem_sem).start()

    barrier = pltpu.get_barrier_semaphore()

    @pl.when(core == 1)
    def _():
        pl.semaphore_signal(barrier, inc=1, device_id=partner, device_id_type=MESH)

    @pl.when(core == 0)
    def _():
        pl.semaphore_wait(barrier, 1)
        pl.semaphore_signal(met, inc=1, device_id=partner, device_id_type=MESH)

    @pl.when(core == 1)
    def _():
        pl.semaphore_wait(met, 1)
        for j, k in order:
            pl.semaphore_signal(barrier, inc=1, device_id=(row_to[j] * 2 + 1, col_to[k]), device_id_type=MESH)

    pltpu.make_async_copy(three_v, three_v, three_sem).wait()
    lane = lax.broadcasted_iota(jnp.int32, (16, 128), 1)
    turned = (128 - row % 8 * 16) % 128
    diagonal = (
        lax.broadcasted_iota(jnp.int32, (128, 128), 0) // 16 == lax.broadcasted_iota(jnp.int32, (128, 128), 1) // 16
    )
    block = []
    for c in range(2):
        piece = three_v[c, 0]
        for x in range(1, 16):
            piece = piece + three_v[c, x]
        piece = jnp.where(lane < 16, pltpu.roll(piece * factor, turned, 1), 0.0)
        for amount in (16, 32, 64):
            piece = piece + pltpu.roll(piece, amount, 1)
        block.append(jnp.where(diagonal, jnp.concatenate([piece] * 8, axis=0), 0.0))
    put_left(k_lhs, block[0], block[1], 128, 128)

    pltpu.make_async_copy(relabel_v, relabel_v, relabel_sem).wait()
    names = jnp.broadcast_to(relabel_v[...].reshape(1, 256), (256, 256))
    pick = jnp.where(lax.broadcasted_iota(jnp.int32, (256, 256), 0) == names, 1.0, 0.0).astype(BF16)
    pltpu.make_async_copy(two_v, two_v, two_sem).wait()
    for half in range(2):
        high, low = (dot(part, pick, NT).astype(BF16) for part in split(two_v[half].reshape(256, 256)))
        for block_at, part in enumerate((high, low)):
            m_rhs[block_at * 256 : block_at * 256 + 256, half * 256 : half * 256 + 256] = part
    m_all = three_dots(k_lhs[:, 0:256], k_lhs[:, 256:512], m_rhs[0:256], m_rhs[256:512], NN)
    stacked = [
        jnp.concatenate([m_all[c * 128 : c * 128 + 128, 0:256], m_all[c * 128 : c * 128 + 128, 256:512]], axis=0)
        for c in range(2)
    ]
    put_three(m_lhs, *stacked)

    pltpu.make_async_copy(one_v, one_v, one_sem).wait()
    put_three(o_lhs, one_v[0].reshape(256, 256), one_v[1].reshape(256, 256))
    pltpu.make_async_copy(stem_v, stem_v, stem_sem).wait()
    put_three(t_rhs, *((stem_v[c, 0] + stem_v[c, 1]) + (stem_v[c, 2] + stem_v[c, 3]) for c in range(2)))
    put_three(s_rhs, *product(o_lhs, t_rhs, NN))
    pltpu.make_async_copy(four, four_v, four_sem).start()

    rows = 128 // PIECES
    w_parts = product(m_lhs, s_rhs, NT)
    for c in range(2):
        w_out[c] = w_parts[c][0:128]
    mine = jnp.stack([w_parts[c][128:256] for c in range(2)])

    def core_copy(p):
        return pltpu.make_async_remote_copy(
            src_ref=w_out.at[:, p * rows : (p + 1) * rows],
            dst_ref=w_in.at[:, p * rows : (p + 1) * rows],
            send_sem=core_send.at[p],
            recv_sem=core_recv.at[p],
            device_id=partner,
            device_id_type=MESH,
        )

    for p in range(PIECES):
        core_copy(p).start()

    @pl.when(core == 1)
    def _():
        pl.semaphore_wait(barrier, 63)
        pl.semaphore_signal(all_met, inc=1, device_id=partner, device_id_type=MESH)

    @pl.when(core == 0)
    def _():
        pl.semaphore_wait(all_met, 1)

    chips = 8 // PIECES
    groups = lax.broadcasted_iota(jnp.int32, (chips, 8, 128), 2) // 32
    for p in range(PIECES):
        core_copy(p).wait_recv()
        added = mine[:, p * rows : (p + 1) * rows] + w_in[:, p * rows : (p + 1) * rows]
        added = added.reshape(2, chips, 2, 8, 256)
        for h in range(2):
            tiles = [added[g // 2, :, g % 2, :, h * 128 : h * 128 + 128] for g in range(4)]
            for q, made in enumerate(regroup(tiles, groups)):
                packed[p * chips : (p + 1) * chips, h * 4 + q] = made
        for j, k in order:
            if j // chips == p:
                pltpu.make_async_remote_copy(
                    src_ref=packed.at[j, k],
                    dst_ref=landed.at[j * 8 + k],
                    send_sem=far_send,
                    recv_sem=far_recv,
                    device_id=(row_to[j] * 2 + core, col_to[k]),
                    device_id_type=MESH,
                ).start()

    pltpu.make_async_copy(four_v, four_v, four_sem).wait()
    for c in range(2):
        f_h[c * 256 : c * 256 + 256], f_l[c * 256 : c * 256 + 256] = split(four_v[c])

    pltpu.make_async_copy(landed.at[0:63], landed.at[0:63], far_recv).wait()
    for k in range(8):
        total = landed[k]
        for j in range(1, 7):
            total = total + landed[j * 8 + k]
        total = total + (landed[56 + k] if k < 7 else packed[7, 7])
        sums[col_from[k]] = total
    group = lax.broadcasted_iota(jnp.int32, (8, 128), 1) // 32
    v = jnp.concatenate(
        [jnp.concatenate(regroup([sums[h * 4 + q] for q in range(4)], group), axis=0) for h in range(2)], axis=1
    )
    v_h, v_l = split(v)
    first = dot(jnp.concatenate([v_h, v_l], axis=0), f_h[...], NT)
    made = first[0:32] + first[32:64] + dot(v_h, f_l[...], NT)
    result = (made[0:16, 0:256] - made[16:32, 256:512], made[0:16, 256:512] + made[16:32, 0:256])
    for c in range(2):
        for b in range(8):
            out[c, b] = result[c][:, b * 32 : b * 32 + 32]

    for p in range(PIECES):
        core_copy(p).wait_send()
    pltpu.make_async_copy(landed.at[0:63], landed.at[0:63], far_send).wait()


def body(stem, branch_one, branch_two, branch_three, branch_four, relabel):
    factor = (stem.shape[3] * lax.axis_size("row")) ** (-0.5)
    any_space = pl.BlockSpec(memory_space=pltpu.HBM)
    dma = pltpu.SemaphoreType.DMA
    made = pl.pallas_call(
        functools.partial(kernel, factor),
        out_shape=pltpu.VMEM((2, 8, 16, 32), F32),
        in_specs=[any_space] * 6,
        out_specs=pl.BlockSpec(memory_space=pltpu.VMEM),
        scratch_shapes=[
            pltpu.VMEM((2, 4, 256, 256), F32),
            pltpu.VMEM((2, 8, 32, 256), F32),
            pltpu.VMEM((2, 2, 8, 16, 256), F32),
            pltpu.VMEM((2, 16, 16, 128), F32),
            pltpu.VMEM((2, 256, 256), F32),
            pltpu.VMEM((256,), jnp.int32),
            pltpu.VMEM((256, 512), BF16),
            pltpu.VMEM((512, 512), BF16),
            *[pltpu.VMEM((3, 2, 256, 256), BF16)] * 4,
            pltpu.VMEM((512, 256), BF16),
            pltpu.VMEM((512, 256), BF16),
            pltpu.VMEM((2, 128, 256), F32),
            pltpu.VMEM((2, 128, 256), F32),
            pltpu.VMEM((8, 8, 8, 128), F32),
            pltpu.VMEM((64, 8, 128), F32),
            pltpu.VMEM((8, 8, 128), F32),
            dma, dma, dma, dma, dma, dma,
            dma((PIECES,)), dma((PIECES,)), dma, dma,
            pltpu.SemaphoreType.REGULAR, pltpu.SemaphoreType.REGULAR,
        ],
        compiler_params=pltpu.CompilerParams(
            collective_id=0, has_side_effects=True, vmem_limit_bytes=40 << 20
        ),
        name="contract",
    )(
        *(
            pltpu.with_memory_space_constraint(value, pltpu.HBM)
            for value in (
                stem.reshape(2, 4, 256, 256),
                branch_one.reshape(2, 8, 32, 256),
                branch_two.reshape(2, 8, 2, 16, 256),
                branch_three.reshape(2, 16, 16, 256),
                branch_four,
                relabel,
            )
        )
    )
    return made.transpose(0, 1, 3, 2)


def solution(mesh):
    in_specs = (P(None, "row", "col", None, None, None), P(), P(), P(), P(), P())
    out_specs = P(None, None, "col", "row")
    return jax.shard_map(body, mesh=mesh, in_specs=in_specs, out_specs=out_specs, check_vma=False)
```

```python
import functools

import jax
import jax.numpy as jnp
from jax import lax
from jax.experimental import pallas as pl
from jax.experimental.pallas import tpu as pltpu
from jax.sharding import PartitionSpec as P

MESH = pl.DeviceIdType.MESH
F32, BF16 = jnp.float32, jnp.bfloat16
NT = (((1,), (1,)), ((), ()))
NN = (((1,), (0,)), ((), ()))

OFFSETS = ((1, 2), (1, 1), (1, 3), (0, 2), (1, 0), (0, 1), (0, 3), (0, 0))
PIECES = 4


def dot(lhs, rhs, dims):
    return lax.dot_general(lhs, rhs, dims, preferred_element_type=F32)


def split(value):
    high = value.astype(BF16)
    return high, (value - high.astype(F32)).astype(BF16)


def hops(j, k):
    (y_hi, x), (y_lo, z) = OFFSETS[j], OFFSETS[k]
    return min(x, 4 - x) + min(z, 4 - z) + (1 if y_lo else 2 * y_hi)


def shifted(index, offset, sign):
    high, low = index // 4, index % 4
    return ((high + 2 + sign * offset[0]) % 2) * 4 + (low + 4 + sign * offset[1]) % 4


def lanes_to(value, source, target):
    amount = (target - source) * 32 % 128
    return value if amount == 0 else pltpu.roll(value, amount, value.ndim - 1)


def regroup(tiles, lane_group):
    out = []
    for j in range(4):
        made = lanes_to(tiles[0], j, 0)
        for i in range(1, 4):
            made = jnp.where(lane_group == i, lanes_to(tiles[i], j, i), made)
        out.append(made)
    return out


def put_left(ref, real_part, imag_part, rows, width, row=0, column=0):
    for block, (re, im) in enumerate(zip(split(real_part), split(imag_part))):
        at = column + block * 2 * width
        ref[row : row + rows, at : at + width] = re
        ref[row : row + rows, at + width : at + 2 * width] = -im
        ref[row + rows : row + 2 * rows, at : at + width] = im
        ref[row + rows : row + 2 * rows, at + width : at + 2 * width] = re


def three_dots(left_high, left_low, right_high, right_low, dims):
    return dot(left_high, right_high, dims) + dot(left_low, right_high, dims) + dot(left_high, right_low, dims)


def put_three(ref, real_part, imag_part):
    for i, value in enumerate((real_part, imag_part, real_part + imag_part)):
        for part, made in enumerate(split(value)):
            ref[i, part] = made


def product(left, right, dims):
    rr, ii, ss = (three_dots(left[i, 0], left[i, 1], right[i, 0], right[i, 1], dims) for i in range(3))
    return rr - ii, ss - rr - ii


def kernel(
    factor, stem, one, two, three, four, relabel, out,
    stem_v, one_v, two_v, three_v, four_v, relabel_v,
    k_lhs, m_rhs, m_lhs, t_rhs, o_lhs, s_rhs, f_h, f_l,
    w_out, w_in, packed, landed, sums,
    stem_sem, one_sem, two_sem, three_sem, four_sem, relabel_sem,
    core_send, core_recv, far_send, far_recv, met, all_met,
):
    row, col = lax.axis_index("row"), lax.axis_index("col")
    chip, core = row // 2, row % 2
    partner = (chip * 2 + 1 - core, col)
    row_to = [shifted(chip, o, 1) for o in OFFSETS]
    col_to = [shifted(col, o, 1) for o in OFFSETS]
    col_from = [shifted(col, o, -1) for o in OFFSETS]
    order = sorted(
        ((j, k) for j in range(8) for k in range(8) if (j, k) != (7, 7)),
        key=lambda jk: -hops(*jk),
    )

    barrier = pltpu.get_barrier_semaphore()

    @pl.when(core == 1)
    def _():
        pl.semaphore_signal(barrier, inc=1, device_id=partner, device_id_type=MESH)

    pltpu.make_async_copy(relabel, relabel_v, relabel_sem).start()
    column = pl.multiple_of(row // 8 * 128, 128)
    for x in range(16):
        pltpu.make_async_copy(three.at[:, x, :, pl.ds(column, 128)], three_v.at[:, x], three_sem).start()
    for j in range(8):
        for half in range(2):
            source = 1 - core if half == 0 else core
            pltpu.make_async_copy(two.at[:, row_to[j], source], two_v.at[half, :, j], two_sem).start()
    for k in range(8):
        pltpu.make_async_copy(one.at[:, col_to[k]], one_v.at[:, k], one_sem).start()
    for c in range(2):
        for f in range(0, 4, 2):
            pltpu.make_async_copy(stem.at[c, f : f + 2], stem_v.at[c, f : f + 2], stem_sem).start(priority=1)

    @pl.when(core == 0)
    def _():
        pl.semaphore_wait(barrier, 1)
        pl.semaphore_signal(met, inc=1, device_id=partner, device_id_type=MESH)

    @pl.when(core == 1)
    def _():
        pl.semaphore_wait(met, 1)
        for j, k in order:
            pl.semaphore_signal(barrier, inc=1, device_id=(row_to[j] * 2 + 1, col_to[k]), device_id_type=MESH)

    pltpu.make_async_copy(three_v, three_v, three_sem).wait()
    lane = lax.broadcasted_iota(jnp.int32, (16, 128), 1)
    turned = (128 - row % 8 * 16) % 128
    diagonal = (
        lax.broadcasted_iota(jnp.int32, (128, 128), 0) // 16 == lax.broadcasted_iota(jnp.int32, (128, 128), 1) // 16
    )
    block = []
    for c in range(2):
        piece = three_v[c, 0]
        for x in range(1, 16):
            piece = piece + three_v[c, x]
        piece = jnp.where(lane < 16, pltpu.roll(piece * factor, turned, 1), 0.0)
        for amount in (16, 32, 64):
            piece = piece + pltpu.roll(piece, amount, 1)
        block.append(jnp.where(diagonal, jnp.concatenate([piece] * 8, axis=0), 0.0))
    put_left(k_lhs, block[0], block[1], 128, 128)

    pltpu.make_async_copy(relabel_v, relabel_v, relabel_sem).wait()
    names = jnp.broadcast_to(relabel_v[...].reshape(1, 256), (256, 256))
    pick = jnp.where(lax.broadcasted_iota(jnp.int32, (256, 256), 0) == names, 1.0, 0.0).astype(BF16)
    pltpu.make_async_copy(two_v, two_v, two_sem).wait()
    for half in range(2):
        high, low = (dot(part, pick, NT).astype(BF16) for part in split(two_v[half].reshape(256, 256)))
        for block_at, part in enumerate((high, low)):
            m_rhs[block_at * 256 : block_at * 256 + 256, half * 256 : half * 256 + 256] = part
    m_all = three_dots(k_lhs[:, 0:256], k_lhs[:, 256:512], m_rhs[0:256], m_rhs[256:512], NN)
    stacked = [
        jnp.concatenate([m_all[c * 128 : c * 128 + 128, 0:256], m_all[c * 128 : c * 128 + 128, 256:512]], axis=0)
        for c in range(2)
    ]
    put_three(m_lhs, *stacked)

    pltpu.make_async_copy(one_v, one_v, one_sem).wait()
    put_three(o_lhs, one_v[0].reshape(256, 256), one_v[1].reshape(256, 256))
    pltpu.make_async_copy(stem_v, stem_v, stem_sem).wait()
    put_three(t_rhs, *((stem_v[c, 0] + stem_v[c, 1]) + (stem_v[c, 2] + stem_v[c, 3]) for c in range(2)))
    put_three(s_rhs, *product(o_lhs, t_rhs, NN))
    pltpu.make_async_copy(four, four_v, four_sem).start()

    rows = 128 // PIECES
    w_parts = product(m_lhs, s_rhs, NT)
    for c in range(2):
        w_out[c] = w_parts[c][0:128]
    mine = jnp.stack([w_parts[c][128:256] for c in range(2)])

    def core_copy(p):
        return pltpu.make_async_remote_copy(
            src_ref=w_out.at[:, p * rows : (p + 1) * rows],
            dst_ref=w_in.at[:, p * rows : (p + 1) * rows],
            send_sem=core_send.at[p],
            recv_sem=core_recv.at[p],
            device_id=partner,
            device_id_type=MESH,
        )

    for p in range(PIECES):
        core_copy(p).start()

    @pl.when(core == 1)
    def _():
        pl.semaphore_wait(barrier, 63)
        pl.semaphore_signal(all_met, inc=1, device_id=partner, device_id_type=MESH)

    @pl.when(core == 0)
    def _():
        pl.semaphore_wait(all_met, 1)

    chips = 8 // PIECES
    groups = lax.broadcasted_iota(jnp.int32, (chips, 8, 128), 2) // 32
    for p in range(PIECES):
        core_copy(p).wait_recv()
        added = mine[:, p * rows : (p + 1) * rows] + w_in[:, p * rows : (p + 1) * rows]
        added = added.reshape(2, chips, 2, 8, 256)
        for h in range(2):
            tiles = [added[g // 2, :, g % 2, :, h * 128 : h * 128 + 128] for g in range(4)]
            for q, made in enumerate(regroup(tiles, groups)):
                packed[p * chips : (p + 1) * chips, h * 4 + q] = made
        for j, k in order:
            if j // chips == p:
                pltpu.make_async_remote_copy(
                    src_ref=packed.at[j, k],
                    dst_ref=landed.at[j * 8 + k],
                    send_sem=far_send,
                    recv_sem=far_recv,
                    device_id=(row_to[j] * 2 + core, col_to[k]),
                    device_id_type=MESH,
                ).start()

    pltpu.make_async_copy(four_v, four_v, four_sem).wait()
    for c in range(2):
        f_h[c * 256 : c * 256 + 256], f_l[c * 256 : c * 256 + 256] = split(four_v[c])

    pltpu.make_async_copy(landed.at[0:63], landed.at[0:63], far_recv).wait()
    for k in range(8):
        total = landed[k]
        for j in range(1, 7):
            total = total + landed[j * 8 + k]
        total = total + (landed[56 + k] if k < 7 else packed[7, 7])
        sums[col_from[k]] = total
    group = lax.broadcasted_iota(jnp.int32, (8, 128), 1) // 32
    v = jnp.concatenate(
        [jnp.concatenate(regroup([sums[h * 4 + q] for q in range(4)], group), axis=0) for h in range(2)], axis=1
    )
    v_h, v_l = split(v)
    first = dot(jnp.concatenate([v_h, v_l], axis=0), f_h[...], NT)
    made = first[0:32] + first[32:64] + dot(v_h, f_l[...], NT)
    result = (made[0:16, 0:256] - made[16:32, 256:512], made[0:16, 256:512] + made[16:32, 0:256])
    for c in range(2):
        for b in range(8):
            out[c, b] = result[c][:, b * 32 : b * 32 + 32]

    for p in range(PIECES):
        core_copy(p).wait_send()
    pltpu.make_async_copy(landed.at[0:63], landed.at[0:63], far_send).wait()


def body(stem, branch_one, branch_two, branch_three, branch_four, relabel):
    factor = (stem.shape[3] * lax.axis_size("row")) ** (-0.5)
    any_space = pl.BlockSpec(memory_space=pltpu.HBM)
    dma = pltpu.SemaphoreType.DMA
    made = pl.pallas_call(
        functools.partial(kernel, factor),
        out_shape=pltpu.VMEM((2, 8, 16, 32), F32),
        in_specs=[any_space] * 6,
        out_specs=pl.BlockSpec(memory_space=pltpu.VMEM),
        scratch_shapes=[
            pltpu.VMEM((2, 4, 256, 256), F32),
            pltpu.VMEM((2, 8, 32, 256), F32),
            pltpu.VMEM((2, 2, 8, 16, 256), F32),
            pltpu.VMEM((2, 16, 16, 128), F32),
            pltpu.VMEM((2, 256, 256), F32),
            pltpu.VMEM((256,), jnp.int32),
            pltpu.VMEM((256, 512), BF16),
            pltpu.VMEM((512, 512), BF16),
            *[pltpu.VMEM((3, 2, 256, 256), BF16)] * 4,
            pltpu.VMEM((512, 256), BF16),
            pltpu.VMEM((512, 256), BF16),
            pltpu.VMEM((2, 128, 256), F32),
            pltpu.VMEM((2, 128, 256), F32),
            pltpu.VMEM((8, 8, 8, 128), F32),
            pltpu.VMEM((64, 8, 128), F32),
            pltpu.VMEM((8, 8, 128), F32),
            dma, dma, dma, dma, dma, dma,
            dma((PIECES,)), dma((PIECES,)), dma, dma,
            pltpu.SemaphoreType.REGULAR, pltpu.SemaphoreType.REGULAR,
        ],
        compiler_params=pltpu.CompilerParams(
            collective_id=0, has_side_effects=True, vmem_limit_bytes=40 << 20
        ),
        name="contract",
    )(
        *(
            pltpu.with_memory_space_constraint(value, pltpu.HBM)
            for value in (
                stem.reshape(2, 4, 256, 256),
                branch_one.reshape(2, 8, 32, 256),
                branch_two.reshape(2, 8, 2, 16, 256),
                branch_three.reshape(2, 16, 16, 256),
                branch_four,
                relabel,
            )
        )
    )
    return made.transpose(0, 1, 3, 2)


def solution(mesh):
    in_specs = (P(None, "row", "col", None, None, None), P(), P(), P(), P(), P())
    out_specs = P(None, None, "col", "row")
    return jax.shard_map(body, mesh=mesh, in_specs=in_specs, out_specs=out_specs, check_vma=False)
```

```python
import functools

import jax
import jax.numpy as jnp
from jax import lax
from jax.experimental import pallas as pl
from jax.experimental.pallas import tpu as pltpu
from jax.sharding import PartitionSpec as P

MESH = pl.DeviceIdType.MESH
F32, BF16 = jnp.float32, jnp.bfloat16
NT = (((1,), (1,)), ((), ()))
NN = (((1,), (0,)), ((), ()))

OFFSETS = ((1, 2), (1, 1), (1, 0), (1, 3), (0, 2), (0, 1), (0, 3), (0, 0))
PIECES = 4
LATE = 5


def dot(lhs, rhs, dims):
    return lax.dot_general(lhs, rhs, dims, preferred_element_type=F32)


def split(value):
    high = value.astype(BF16)
    return high, (value - high.astype(F32)).astype(BF16)


def hops(j, k):
    (y_hi, x), (y_lo, z) = OFFSETS[j], OFFSETS[k]
    return min(x, 4 - x) + min(z, 4 - z) + (1 if y_lo else 2 * y_hi)


def shifted(index, offset, sign):
    high, low = index // 4, index % 4
    return ((high + 2 + sign * offset[0]) % 2) * 4 + (low + 4 + sign * offset[1]) % 4


def lanes_to(value, source, target):
    amount = (target - source) * 32 % 128
    return value if amount == 0 else pltpu.roll(value, amount, value.ndim - 1)


def regroup(tiles, lane_group):
    out = []
    for j in range(4):
        made = lanes_to(tiles[0], j, 0)
        for i in range(1, 4):
            made = jnp.where(lane_group == i, lanes_to(tiles[i], j, i), made)
        out.append(made)
    return out


def put_left(ref, real_part, imag_part, rows, width, row=0, column=0):
    for block, (re, im) in enumerate(zip(split(real_part), split(imag_part))):
        at = column + block * 2 * width
        ref[row : row + rows, at : at + width] = re
        ref[row : row + rows, at + width : at + 2 * width] = -im
        ref[row + rows : row + 2 * rows, at : at + width] = im
        ref[row + rows : row + 2 * rows, at + width : at + 2 * width] = re


def three_dots(left_high, left_low, right_high, right_low, dims):
    return dot(left_high, right_high, dims) + dot(left_low, right_high, dims) + dot(left_high, right_low, dims)


def put_three(ref, real_part, imag_part):
    for i, value in enumerate((real_part, imag_part, real_part + imag_part)):
        for part, made in enumerate(split(value)):
            ref[i, part] = made


def product(left, right, dims):
    rr, ii, ss = (three_dots(left[i, 0], left[i, 1], right[i, 0], right[i, 1], dims) for i in range(3))
    return rr - ii, ss - rr - ii


def kernel(
    factor, stem, one, two, three, four, relabel, out,
    stem_v, one_v, two_v, three_v, four_v, relabel_v,
    k_lhs, m_rhs, m_lhs, t_rhs, o_lhs, s_rhs, f_h, f_l,
    w_out, w_in, packed, landed,
    stem_sem, one_sem, two_sem, three_sem, four_sem, relabel_sem,
    core_send, core_recv, far_send, far_recv, met, all_met,
):
    row, col = lax.axis_index("row"), lax.axis_index("col")
    chip, core = row // 2, row % 2
    partner = (chip * 2 + 1 - core, col)
    row_to = [shifted(chip, o, 1) for o in OFFSETS]
    col_to = [shifted(col, o, 1) for o in OFFSETS]
    col_from = [shifted(col, o, -1) for o in OFFSETS]
    order = sorted(
        ((j, k) for j in range(8) for k in range(8) if (j, k) != (7, 7)),
        key=lambda jk: -hops(*jk),
    )
    x, y, z = chip % 4, chip // 4 * 2 + col // 4, col % 4
    late = jnp.minimum(x, 4 - x) + jnp.minimum(y, 4 - y) + z >= LATE

    barrier = pltpu.get_barrier_semaphore()

    @pl.when(core == 1)
    def _():
        pl.semaphore_signal(barrier, inc=1, device_id=partner, device_id_type=MESH)

    pltpu.make_async_copy(relabel, relabel_v, relabel_sem).start()
    column = pl.multiple_of(row // 8 * 128, 128)
    for x in range(16):
        pltpu.make_async_copy(three.at[:, x, :, pl.ds(column, 128)], three_v.at[:, x], three_sem).start()
    @pl.when(core == 0)
    def _():
        pl.semaphore_wait(barrier, 1)
        pl.semaphore_signal(met, inc=1, device_id=partner, device_id_type=MESH)

    for j in range(8):
        for half in range(2):
            source = 1 - core if half == 0 else core
            pltpu.make_async_copy(two.at[:, row_to[j], source], two_v.at[half, :, j], two_sem).start()
    for k in range(8):
        pltpu.make_async_copy(one.at[:, col_to[k]], one_v.at[:, k], one_sem).start()
    for c in range(2):
        for f in range(0, 4, 2):
            pltpu.make_async_copy(stem.at[c, f : f + 2], stem_v.at[c, f : f + 2], stem_sem).start(priority=1)

    @pl.when(core == 1)
    def _():
        pl.semaphore_wait(met, 1)
        for j, k in order:
            pl.semaphore_signal(barrier, inc=1, device_id=(row_to[j] * 2 + 1, col_to[k]), device_id_type=MESH)

    pltpu.make_async_copy(three_v, three_v, three_sem).wait()
    lane = lax.broadcasted_iota(jnp.int32, (16, 128), 1)
    turned = (128 - row % 8 * 16) % 128
    diagonal = (
        lax.broadcasted_iota(jnp.int32, (128, 128), 0) // 16 == lax.broadcasted_iota(jnp.int32, (128, 128), 1) // 16
    )
    block = []
    for c in range(2):
        piece = three_v[c, 0]
        for x in range(1, 16):
            piece = piece + three_v[c, x]
        piece = jnp.where(lane < 16, pltpu.roll(piece * factor, turned, 1), 0.0)
        for amount in (16, 32, 64):
            piece = piece + pltpu.roll(piece, amount, 1)
        block.append(jnp.where(diagonal, jnp.concatenate([piece] * 8, axis=0), 0.0))
    put_left(k_lhs, block[0], block[1], 128, 128)

    pltpu.make_async_copy(relabel_v, relabel_v, relabel_sem).wait()
    names = jnp.broadcast_to(relabel_v[...].reshape(1, 256), (256, 256))
    pick = jnp.where(lax.broadcasted_iota(jnp.int32, (256, 256), 0) == names, 1.0, 0.0).astype(BF16)
    pltpu.make_async_copy(two_v, two_v, two_sem).wait()
    for half in range(2):
        high, low = (dot(part, pick, NT).astype(BF16) for part in split(two_v[half].reshape(256, 256)))
        for block_at, part in enumerate((high, low)):
            m_rhs[block_at * 256 : block_at * 256 + 256, half * 256 : half * 256 + 256] = part
    m_all = three_dots(k_lhs[:, 0:256], k_lhs[:, 256:512], m_rhs[0:256], m_rhs[256:512], NN)
    stacked = [
        jnp.concatenate([m_all[c * 128 : c * 128 + 128, 0:256], m_all[c * 128 : c * 128 + 128, 256:512]], axis=0)
        for c in range(2)
    ]
    put_three(m_lhs, *stacked)

    pltpu.make_async_copy(one_v, one_v, one_sem).wait()
    put_three(o_lhs, one_v[0].reshape(256, 256), one_v[1].reshape(256, 256))
    pltpu.make_async_copy(stem_v, stem_v, stem_sem).wait()
    put_three(t_rhs, *((stem_v[c, 0] + stem_v[c, 1]) + (stem_v[c, 2] + stem_v[c, 3]) for c in range(2)))
    put_three(s_rhs, *product(o_lhs, t_rhs, NN))
    pltpu.make_async_copy(four, four_v, four_sem).start()

    rows = 128 // PIECES
    w_parts = product(m_lhs, s_rhs, NT)
    for c in range(2):
        w_out[c] = w_parts[c][0:128]
    mine = jnp.stack([w_parts[c][128:256] for c in range(2)])

    def core_copy(p):
        return pltpu.make_async_remote_copy(
            src_ref=w_out.at[:, p * rows : (p + 1) * rows],
            dst_ref=w_in.at[:, p * rows : (p + 1) * rows],
            send_sem=core_send.at[p],
            recv_sem=core_recv.at[p],
            device_id=partner,
            device_id_type=MESH,
        )

    for p in range(PIECES):
        core_copy(p).start()

    def wait_for_far(condition):
        @pl.when((core == 1) & condition)
        def _():
            pl.semaphore_wait(barrier, 63)
            pl.semaphore_signal(all_met, inc=1, device_id=partner, device_id_type=MESH)

        @pl.when((core == 0) & condition)
        def _():
            pl.semaphore_wait(all_met, 1)

    def send(j, k):
        pltpu.make_async_remote_copy(
            src_ref=packed.at[j, k],
            dst_ref=landed.at[j * 8 + k],
            send_sem=far_send,
            recv_sem=far_recv,
            device_id=(row_to[j] * 2 + core, col_to[k]),
            device_id_type=MESH,
        ).start()

    wait_for_far(late)

    chips = 8 // PIECES
    groups = lax.broadcasted_iota(jnp.int32, (chips, 8, 128), 2) // 32
    for p in range(PIECES):
        core_copy(p).wait_recv()
        added = mine[:, p * rows : (p + 1) * rows] + w_in[:, p * rows : (p + 1) * rows]
        added = added.reshape(2, chips, 2, 8, 256)
        for h in range(2):
            tiles = [added[g // 2, :, g % 2, :, h * 128 : h * 128 + 128] for g in range(4)]
            for q, made in enumerate(regroup(tiles, groups)):
                packed[p * chips : (p + 1) * chips, h * 4 + q] = made

        @pl.when(late)
        def _():
            for j, k in order:
                if j // chips == p:
                    send(j, k)

    early = jnp.logical_not(late)
    wait_for_far(early)

    @pl.when(early)
    def _():
        for j, k in order:
            send(j, k)

    pltpu.make_async_copy(four_v, four_v, four_sem).wait()
    low = lax.broadcasted_iota(jnp.int32, (32, 256), 0)
    lane = lax.broadcasted_iota(jnp.int32, (32, 256), 1)
    turn = jnp.concatenate([jnp.where(lane == low + col_from[k] * 32, 1.0, 0.0) for k in range(8)], axis=0).astype(BF16)
    for c in range(2):
        for ref, part in zip((f_h, f_l), split(four_v[c])):
            ref[:, c * 256 : c * 256 + 256] = dot(turn, part, NT).astype(BF16)

    pltpu.make_async_copy(landed.at[0:63], landed.at[0:63], far_recv).wait()
    totals = []
    for k in range(8):
        total = landed[k]
        for j in range(1, 7):
            total = total + landed[j * 8 + k]
        total = total + (landed[56 + k] if k < 7 else packed[7, 7])
        totals.append(total)
    group = lax.broadcasted_iota(jnp.int32, (8, 128), 1) // 32
    v = jnp.concatenate(
        [jnp.concatenate(regroup(totals[h * 4 : h * 4 + 4], group), axis=0) for h in range(2)], axis=1
    )
    v_h, v_l = split(v)
    first = dot(jnp.concatenate([v_h, v_l], axis=0), f_h[...], NN)
    made = first[0:32] + first[32:64] + dot(v_h, f_l[...], NN)
    result = (made[0:16, 0:256] - made[16:32, 256:512], made[0:16, 256:512] + made[16:32, 0:256])
    for c in range(2):
        for b in range(8):
            out[c, b] = result[c][:, b * 32 : b * 32 + 32]

    for p in range(PIECES):
        core_copy(p).wait_send()
    pltpu.make_async_copy(landed.at[0:63], landed.at[0:63], far_send).wait()


def body(stem, branch_one, branch_two, branch_three, branch_four, relabel):
    factor = (stem.shape[3] * lax.axis_size("row")) ** (-0.5)
    any_space = pl.BlockSpec(memory_space=pltpu.HBM)
    dma = pltpu.SemaphoreType.DMA
    made = pl.pallas_call(
        functools.partial(kernel, factor),
        out_shape=pltpu.VMEM((2, 8, 16, 32), F32),
        in_specs=[any_space] * 6,
        out_specs=pl.BlockSpec(memory_space=pltpu.VMEM),
        scratch_shapes=[
            pltpu.VMEM((2, 4, 256, 256), F32),
            pltpu.VMEM((2, 8, 32, 256), F32),
            pltpu.VMEM((2, 2, 8, 16, 256), F32),
            pltpu.VMEM((2, 16, 16, 128), F32),
            pltpu.VMEM((2, 256, 256), F32),
            pltpu.VMEM((256,), jnp.int32),
            pltpu.VMEM((256, 512), BF16),
            pltpu.VMEM((512, 512), BF16),
            *[pltpu.VMEM((3, 2, 256, 256), BF16)] * 4,
            pltpu.VMEM((256, 512), BF16),
            pltpu.VMEM((256, 512), BF16),
            pltpu.VMEM((2, 128, 256), F32),
            pltpu.VMEM((2, 128, 256), F32),
            pltpu.VMEM((8, 8, 8, 128), F32),
            pltpu.VMEM((64, 8, 128), F32),
            dma, dma, dma, dma, dma, dma,
            dma((PIECES,)), dma((PIECES,)), dma, dma,
            pltpu.SemaphoreType.REGULAR, pltpu.SemaphoreType.REGULAR,
        ],
        compiler_params=pltpu.CompilerParams(
            collective_id=0, has_side_effects=True, vmem_limit_bytes=40 << 20
        ),
        name="contract",
    )(
        *(
            pltpu.with_memory_space_constraint(value, pltpu.HBM)
            for value in (
                stem.reshape(2, 4, 256, 256),
                branch_one.reshape(2, 8, 32, 256),
                branch_two.reshape(2, 8, 2, 16, 256),
                branch_three.reshape(2, 16, 16, 256),
                branch_four,
                relabel,
            )
        )
    )
    return made.transpose(0, 1, 3, 2)


def solution(mesh):
    in_specs = (P(None, "row", "col", None, None, None), P(), P(), P(), P(), P())
    out_specs = P(None, None, "col", "row")
    return jax.shard_map(body, mesh=mesh, in_specs=in_specs, out_specs=out_specs, check_vma=False)
```

```python
import functools

import jax
import jax.numpy as jnp
from jax import lax
from jax.experimental import pallas as pl
from jax.experimental.pallas import tpu as pltpu
from jax.sharding import PartitionSpec as P

MESH = pl.DeviceIdType.MESH
F32, BF16 = jnp.float32, jnp.bfloat16
NT = (((1,), (1,)), ((), ()))
NN = (((1,), (0,)), ((), ()))

OFFSETS = ((1, 2), (1, 1), (1, 0), (1, 3), (0, 2), (0, 1), (0, 3), (0, 0))
PIECES = 4
LATE = 5


def dot(lhs, rhs, dims):
    return lax.dot_general(lhs, rhs, dims, preferred_element_type=F32)


def split(value):
    high = value.astype(BF16)
    return high, (value - high.astype(F32)).astype(BF16)


def hops(j, k):
    (y_hi, x), (y_lo, z) = OFFSETS[j], OFFSETS[k]
    return min(x, 4 - x) + min(z, 4 - z) + (1 if y_lo else 2 * y_hi)


def shifted(index, offset, sign):
    high, low = index // 4, index % 4
    return ((high + 2 + sign * offset[0]) % 2) * 4 + (low + 4 + sign * offset[1]) % 4


def lanes_to(value, source, target):
    amount = (target - source) * 32 % 128
    return value if amount == 0 else pltpu.roll(value, amount, value.ndim - 1)


def regroup(tiles, lane_group):
    out = []
    for j in range(4):
        made = lanes_to(tiles[0], j, 0)
        for i in range(1, 4):
            made = jnp.where(lane_group == i, lanes_to(tiles[i], j, i), made)
        out.append(made)
    return out


def put_left(ref, real_part, imag_part, rows, width, row=0, column=0):
    for block, (re, im) in enumerate(zip(split(real_part), split(imag_part))):
        at = column + block * 2 * width
        ref[row : row + rows, at : at + width] = re
        ref[row : row + rows, at + width : at + 2 * width] = -im
        ref[row + rows : row + 2 * rows, at : at + width] = im
        ref[row + rows : row + 2 * rows, at + width : at + 2 * width] = re


def three_dots(left_high, left_low, right_high, right_low, dims):
    return dot(left_high, right_high, dims) + dot(left_low, right_high, dims) + dot(left_high, right_low, dims)


def put_three(ref, real_part, imag_part):
    for i, value in enumerate((real_part, imag_part, real_part + imag_part)):
        for part, made in enumerate(split(value)):
            ref[i, part] = made


def product(left, right, dims):
    rr, ii, ss = (three_dots(left[i, 0], left[i, 1], right[i, 0], right[i, 1], dims) for i in range(3))
    return rr - ii, ss - rr - ii


def kernel(
    factor, stem, one, two, three, four, relabel, out,
    stem_v, one_v, two_v, three_v, four_v, relabel_v,
    k_lhs, m_rhs, m_lhs, t_rhs, o_lhs, s_rhs, f_h, f_l,
    w_out, w_in, packed, landed,
    stem_sem, one_sem, two_sem, three_sem, four_sem, relabel_sem,
    core_send, core_recv, far_send, far_recv, met, all_met,
):
    row, col = lax.axis_index("row"), lax.axis_index("col")
    chip, core = row // 2, row % 2
    partner = (chip * 2 + 1 - core, col)
    row_to = [shifted(chip, o, 1) for o in OFFSETS]
    col_to = [shifted(col, o, 1) for o in OFFSETS]
    col_from = [shifted(col, o, -1) for o in OFFSETS]
    order = sorted(
        ((j, k) for j in range(8) for k in range(8) if (j, k) != (7, 7)),
        key=lambda jk: -hops(*jk),
    )
    x, y, z = chip % 4, chip // 4 * 2 + col // 4, col % 4
    late = jnp.minimum(x, 4 - x) + jnp.minimum(y, 4 - y) + z >= LATE

    barrier = pltpu.get_barrier_semaphore()

    @pl.when(core == 1)
    def _():
        pl.semaphore_signal(barrier, inc=1, device_id=partner, device_id_type=MESH)

    pltpu.make_async_copy(relabel, relabel_v, relabel_sem).start()
    column = pl.multiple_of(row // 8 * 128, 128)
    for x in range(16):
        pltpu.make_async_copy(three.at[:, x, :, pl.ds(column, 128)], three_v.at[:, x], three_sem).start()
    @pl.when(core == 0)
    def _():
        pl.semaphore_wait(barrier, 1)
        pl.semaphore_signal(met, inc=1, device_id=partner, device_id_type=MESH)

    for j in range(8):
        for half in range(2):
            source = 1 - core if half == 0 else core
            pltpu.make_async_copy(two.at[:, row_to[j], source], two_v.at[half, :, j], two_sem).start()
    for k in range(8):
        pltpu.make_async_copy(one.at[:, col_to[k]], one_v.at[:, k], one_sem).start()
    for c in range(2):
        for f in range(0, 4, 2):
            pltpu.make_async_copy(stem.at[c, f : f + 2], stem_v.at[c, f : f + 2], stem_sem).start(priority=1)

    @pl.when(core == 1)
    def _():
        pl.semaphore_wait(met, 1)
        for j, k in order:
            pl.semaphore_signal(barrier, inc=1, device_id=(row_to[j] * 2 + 1, col_to[k]), device_id_type=MESH)

    pltpu.make_async_copy(three_v, three_v, three_sem).wait()
    lane = lax.broadcasted_iota(jnp.int32, (16, 128), 1)
    turned = (128 - row % 8 * 16) % 128
    diagonal = (
        lax.broadcasted_iota(jnp.int32, (128, 128), 0) // 16 == lax.broadcasted_iota(jnp.int32, (128, 128), 1) // 16
    )
    block = []
    for c in range(2):
        piece = three_v[c, 0]
        for x in range(1, 16):
            piece = piece + three_v[c, x]
        piece = jnp.where(lane < 16, pltpu.roll(piece * factor, turned, 1), 0.0)
        for amount in (16, 32, 64):
            piece = piece + pltpu.roll(piece, amount, 1)
        block.append(jnp.where(diagonal, jnp.concatenate([piece] * 8, axis=0), 0.0))
    put_left(k_lhs, block[0], block[1], 128, 128)

    pltpu.make_async_copy(relabel_v, relabel_v, relabel_sem).wait()
    names = jnp.broadcast_to(relabel_v[...].reshape(1, 256), (256, 256))
    pick = jnp.where(lax.broadcasted_iota(jnp.int32, (256, 256), 0) == names, 1.0, 0.0).astype(BF16)
    pltpu.make_async_copy(two_v, two_v, two_sem).wait()
    for half in range(2):
        high, low = (dot(part, pick, NT).astype(BF16) for part in split(two_v[half].reshape(256, 256)))
        for block_at, part in enumerate((high, low)):
            m_rhs[block_at * 256 : block_at * 256 + 256, half * 256 : half * 256 + 256] = part
    m_all = three_dots(k_lhs[:, 0:256], k_lhs[:, 256:512], m_rhs[0:256], m_rhs[256:512], NN)
    stacked = [
        jnp.concatenate([m_all[c * 128 : c * 128 + 128, 0:256], m_all[c * 128 : c * 128 + 128, 256:512]], axis=0)
        for c in range(2)
    ]
    put_three(m_lhs, *stacked)

    pltpu.make_async_copy(one_v, one_v, one_sem).wait()
    put_three(o_lhs, one_v[0].reshape(256, 256), one_v[1].reshape(256, 256))
    pltpu.make_async_copy(stem_v, stem_v, stem_sem).wait()
    put_three(t_rhs, *((stem_v[c, 0] + stem_v[c, 1]) + (stem_v[c, 2] + stem_v[c, 3]) for c in range(2)))
    put_three(s_rhs, *product(o_lhs, t_rhs, NN))
    pltpu.make_async_copy(four, four_v, four_sem).start()

    rows = 128 // PIECES
    w_parts = product(m_lhs, s_rhs, NT)
    for c in range(2):
        w_out[c] = w_parts[c][0:128]
    mine = jnp.stack([w_parts[c][128:256] for c in range(2)])

    def core_copy(p):
        return pltpu.make_async_remote_copy(
            src_ref=w_out.at[:, p * rows : (p + 1) * rows],
            dst_ref=w_in.at[:, p * rows : (p + 1) * rows],
            send_sem=core_send.at[p],
            recv_sem=core_recv.at[p],
            device_id=partner,
            device_id_type=MESH,
        )

    for p in range(PIECES):
        core_copy(p).start()

    def wait_for_far(condition):
        @pl.when((core == 1) & condition)
        def _():
            pl.semaphore_wait(barrier, 63)
            pl.semaphore_signal(all_met, inc=1, device_id=partner, device_id_type=MESH)

        @pl.when((core == 0) & condition)
        def _():
            pl.semaphore_wait(all_met, 1)

    def send(j, k):
        pltpu.make_async_remote_copy(
            src_ref=packed.at[j, k],
            dst_ref=landed.at[j * 8 + k],
            send_sem=far_send,
            recv_sem=far_recv,
            device_id=(row_to[j] * 2 + core, col_to[k]),
            device_id_type=MESH,
        ).start()

    chips = 8 // PIECES
    groups = lax.broadcasted_iota(jnp.int32, (chips, 8, 128), 2) // 32
    for p in range(PIECES):
        core_copy(p).wait_recv()
        added = mine[:, p * rows : (p + 1) * rows] + w_in[:, p * rows : (p + 1) * rows]
        added = added.reshape(2, chips, 2, 8, 256)
        for h in range(2):
            tiles = [added[g // 2, :, g % 2, :, h * 128 : h * 128 + 128] for g in range(4)]
            for q, made in enumerate(regroup(tiles, groups)):
                packed[p * chips : (p + 1) * chips, h * 4 + q] = made

        if p == 0:
            wait_for_far(late)

        @pl.when(late)
        def _():
            for j, k in order:
                if j // chips == p:
                    send(j, k)

    early = jnp.logical_not(late)
    wait_for_far(early)

    @pl.when(early)
    def _():
        for j, k in order:
            send(j, k)

    pltpu.make_async_copy(four_v, four_v, four_sem).wait()
    low = lax.broadcasted_iota(jnp.int32, (32, 256), 0)
    lane = lax.broadcasted_iota(jnp.int32, (32, 256), 1)
    turn = jnp.concatenate([jnp.where(lane == low + col_from[k] * 32, 1.0, 0.0) for k in range(8)], axis=0).astype(BF16)
    for c in range(2):
        for ref, part in zip((f_h, f_l), split(four_v[c])):
            ref[:, c * 256 : c * 256 + 256] = dot(turn, part, NT).astype(BF16)

    pltpu.make_async_copy(landed.at[0:63], landed.at[0:63], far_recv).wait()
    totals = []
    for k in range(8):
        total = landed[k]
        for j in range(1, 7):
            total = total + landed[j * 8 + k]
        total = total + (landed[56 + k] if k < 7 else packed[7, 7])
        totals.append(total)
    group = lax.broadcasted_iota(jnp.int32, (8, 128), 1) // 32
    v = jnp.concatenate(
        [jnp.concatenate(regroup(totals[h * 4 : h * 4 + 4], group), axis=0) for h in range(2)], axis=1
    )
    v_h, v_l = split(v)
    first = dot(jnp.concatenate([v_h, v_l], axis=0), f_h[...], NN)
    made = first[0:32] + first[32:64] + dot(v_h, f_l[...], NN)
    result = (made[0:16, 0:256] - made[16:32, 256:512], made[0:16, 256:512] + made[16:32, 0:256])
    for c in range(2):
        for b in range(8):
            out[c, b] = result[c][:, b * 32 : b * 32 + 32]

    for p in range(PIECES):
        core_copy(p).wait_send()
    pltpu.make_async_copy(landed.at[0:63], landed.at[0:63], far_send).wait()


def body(stem, branch_one, branch_two, branch_three, branch_four, relabel):
    factor = (stem.shape[3] * lax.axis_size("row")) ** (-0.5)
    any_space = pl.BlockSpec(memory_space=pltpu.HBM)
    dma = pltpu.SemaphoreType.DMA
    made = pl.pallas_call(
        functools.partial(kernel, factor),
        out_shape=pltpu.VMEM((2, 8, 16, 32), F32),
        in_specs=[any_space] * 6,
        out_specs=pl.BlockSpec(memory_space=pltpu.VMEM),
        scratch_shapes=[
            pltpu.VMEM((2, 4, 256, 256), F32),
            pltpu.VMEM((2, 8, 32, 256), F32),
            pltpu.VMEM((2, 2, 8, 16, 256), F32),
            pltpu.VMEM((2, 16, 16, 128), F32),
            pltpu.VMEM((2, 256, 256), F32),
            pltpu.VMEM((256,), jnp.int32),
            pltpu.VMEM((256, 512), BF16),
            pltpu.VMEM((512, 512), BF16),
            *[pltpu.VMEM((3, 2, 256, 256), BF16)] * 4,
            pltpu.VMEM((256, 512), BF16),
            pltpu.VMEM((256, 512), BF16),
            pltpu.VMEM((2, 128, 256), F32),
            pltpu.VMEM((2, 128, 256), F32),
            pltpu.VMEM((8, 8, 8, 128), F32),
            pltpu.VMEM((64, 8, 128), F32),
            dma, dma, dma, dma, dma, dma,
            dma((PIECES,)), dma((PIECES,)), dma, dma,
            pltpu.SemaphoreType.REGULAR, pltpu.SemaphoreType.REGULAR,
        ],
        compiler_params=pltpu.CompilerParams(
            collective_id=0, has_side_effects=True, vmem_limit_bytes=40 << 20
        ),
        name="contract",
    )(
        *(
            pltpu.with_memory_space_constraint(value, pltpu.HBM)
            for value in (
                stem.reshape(2, 4, 256, 256),
                branch_one.reshape(2, 8, 32, 256),
                branch_two.reshape(2, 8, 2, 16, 256),
                branch_three.reshape(2, 16, 16, 256),
                branch_four,
                relabel,
            )
        )
    )
    return made.transpose(0, 1, 3, 2)


def solution(mesh):
    in_specs = (P(None, "row", "col", None, None, None), P(), P(), P(), P(), P())
    out_specs = P(None, None, "col", "row")
    return jax.shard_map(body, mesh=mesh, in_specs=in_specs, out_specs=out_specs, check_vma=False)
```

```python
import functools

import jax
import jax.numpy as jnp
from jax import lax
from jax.experimental import pallas as pl
from jax.experimental.pallas import tpu as pltpu
from jax.sharding import PartitionSpec as P

MESH = pl.DeviceIdType.MESH
F32, BF16 = jnp.float32, jnp.bfloat16
NT = (((1,), (1,)), ((), ()))
NN = (((1,), (0,)), ((), ()))

OFFSETS = ((1, 2), (1, 1), (1, 0), (1, 3), (0, 2), (0, 1), (0, 3), (0, 0))
PIECES = 4


def dot(lhs, rhs, dims):
    return lax.dot_general(lhs, rhs, dims, preferred_element_type=F32)


def split(value):
    high = value.astype(BF16)
    return high, (value - high.astype(F32)).astype(BF16)


def hops(j, k):
    (y_hi, x), (y_lo, z) = OFFSETS[j], OFFSETS[k]
    return min(x, 4 - x) + min(z, 4 - z) + (1 if y_lo else 2 * y_hi)


def shifted(index, offset, sign):
    high, low = index // 4, index % 4
    return ((high + 2 + sign * offset[0]) % 2) * 4 + (low + 4 + sign * offset[1]) % 4


def lanes_to(value, source, target):
    amount = (target - source) * 32 % 128
    return value if amount == 0 else pltpu.roll(value, amount, value.ndim - 1)


def regroup(tiles, lane_group):
    out = []
    for j in range(4):
        made = lanes_to(tiles[0], j, 0)
        for i in range(1, 4):
            made = jnp.where(lane_group == i, lanes_to(tiles[i], j, i), made)
        out.append(made)
    return out


def put_left(ref, real_part, imag_part, rows, width, row=0, column=0):
    for block, (re, im) in enumerate(zip(split(real_part), split(imag_part))):
        at = column + block * 2 * width
        ref[row : row + rows, at : at + width] = re
        ref[row : row + rows, at + width : at + 2 * width] = -im
        ref[row + rows : row + 2 * rows, at : at + width] = im
        ref[row + rows : row + 2 * rows, at + width : at + 2 * width] = re


def three_dots(left_high, left_low, right_high, right_low, dims):
    return dot(left_high, right_high, dims) + dot(left_low, right_high, dims) + dot(left_high, right_low, dims)


def put_three(ref, real_part, imag_part):
    for i, value in enumerate((real_part, imag_part, real_part + imag_part)):
        for part, made in enumerate(split(value)):
            ref[i, part] = made


def product(left, right, dims):
    rr, ii, ss = (three_dots(left[i, 0], left[i, 1], right[i, 0], right[i, 1], dims) for i in range(3))
    return rr - ii, ss - rr - ii


def kernel(
    factor, stem, one, two, three, four, relabel, out,
    stem_v, one_v, two_v, three_v, four_v, relabel_v,
    k_lhs, m_rhs, m_lhs, t_rhs, o_lhs, s_rhs, f_h, f_l,
    w_out, w_in, packed, landed, sums,
    stem_sem, one_sem, two_sem, three_sem, four_sem, relabel_sem,
    core_send, core_recv, far_send, far_recv, met, all_met,
):
    row, col = lax.axis_index("row"), lax.axis_index("col")
    chip, core = row // 2, row % 2
    partner = (chip * 2 + 1 - core, col)
    row_to = [shifted(chip, o, 1) for o in OFFSETS]
    col_to = [shifted(col, o, 1) for o in OFFSETS]
    col_from = [shifted(col, o, -1) for o in OFFSETS]
    order = sorted(
        ((j, k) for j in range(8) for k in range(8) if (j, k) != (7, 7)),
        key=lambda jk: -hops(*jk),
    )

    barrier = pltpu.get_barrier_semaphore()

    @pl.when(core == 1)
    def _():
        pl.semaphore_signal(barrier, inc=1, device_id=partner, device_id_type=MESH)

    pltpu.make_async_copy(relabel, relabel_v, relabel_sem).start()
    column = pl.multiple_of(row // 8 * 128, 128)
    for x in range(16):
        pltpu.make_async_copy(three.at[:, x, :, pl.ds(column, 128)], three_v.at[:, x], three_sem).start()
    for j in range(8):
        for half in range(2):
            source = 1 - core if half == 0 else core
            pltpu.make_async_copy(two.at[:, row_to[j], source], two_v.at[half, :, j], two_sem).start()
    for k in range(8):
        pltpu.make_async_copy(one.at[:, col_to[k]], one_v.at[:, k], one_sem).start()
    for c in range(2):
        for f in range(0, 4, 2):
            pltpu.make_async_copy(stem.at[c, f : f + 2], stem_v.at[c, f : f + 2], stem_sem).start(priority=1)

    @pl.when(core == 0)
    def _():
        pl.semaphore_wait(barrier, 1)
        pl.semaphore_signal(met, inc=1, device_id=partner, device_id_type=MESH)

    @pl.when(core == 1)
    def _():
        pl.semaphore_wait(met, 1)
        for j, k in order:
            pl.semaphore_signal(barrier, inc=1, device_id=(row_to[j] * 2 + 1, col_to[k]), device_id_type=MESH)

    pltpu.make_async_copy(three_v, three_v, three_sem).wait()
    lane = lax.broadcasted_iota(jnp.int32, (16, 128), 1)
    turned = (128 - row % 8 * 16) % 128
    diagonal = (
        lax.broadcasted_iota(jnp.int32, (128, 128), 0) // 16 == lax.broadcasted_iota(jnp.int32, (128, 128), 1) // 16
    )
    block = []
    for c in range(2):
        piece = three_v[c, 0]
        for x in range(1, 16):
            piece = piece + three_v[c, x]
        piece = jnp.where(lane < 16, pltpu.roll(piece * factor, turned, 1), 0.0)
        for amount in (16, 32, 64):
            piece = piece + pltpu.roll(piece, amount, 1)
        block.append(jnp.where(diagonal, jnp.concatenate([piece] * 8, axis=0), 0.0))
    put_left(k_lhs, block[0], block[1], 128, 128)

    pltpu.make_async_copy(relabel_v, relabel_v, relabel_sem).wait()
    names = jnp.broadcast_to(relabel_v[...].reshape(1, 256), (256, 256))
    pick = jnp.where(lax.broadcasted_iota(jnp.int32, (256, 256), 0) == names, 1.0, 0.0).astype(BF16)
    pltpu.make_async_copy(two_v, two_v, two_sem).wait()
    for half in range(2):
        high, low = (dot(part, pick, NT).astype(BF16) for part in split(two_v[half].reshape(256, 256)))
        for block_at, part in enumerate((high, low)):
            m_rhs[block_at * 256 : block_at * 256 + 256, half * 256 : half * 256 + 256] = part
    m_all = three_dots(k_lhs[:, 0:256], k_lhs[:, 256:512], m_rhs[0:256], m_rhs[256:512], NN)
    stacked = [
        jnp.concatenate([m_all[c * 128 : c * 128 + 128, 0:256], m_all[c * 128 : c * 128 + 128, 256:512]], axis=0)
        for c in range(2)
    ]
    put_three(m_lhs, *stacked)

    pltpu.make_async_copy(one_v, one_v, one_sem).wait()
    put_three(o_lhs, one_v[0].reshape(256, 256), one_v[1].reshape(256, 256))
    pltpu.make_async_copy(stem_v, stem_v, stem_sem).wait()
    put_three(t_rhs, *((stem_v[c, 0] + stem_v[c, 1]) + (stem_v[c, 2] + stem_v[c, 3]) for c in range(2)))
    put_three(s_rhs, *product(o_lhs, t_rhs, NN))
    pltpu.make_async_copy(four, four_v, four_sem).start()

    rows = 128 // PIECES
    w_parts = product(m_lhs, s_rhs, NT)
    for c in range(2):
        w_out[c] = w_parts[c][0:128]
    mine = jnp.stack([w_parts[c][128:256] for c in range(2)])

    def core_copy(p):
        return pltpu.make_async_remote_copy(
            src_ref=w_out.at[:, p * rows : (p + 1) * rows],
            dst_ref=w_in.at[:, p * rows : (p + 1) * rows],
            send_sem=core_send.at[p],
            recv_sem=core_recv.at[p],
            device_id=partner,
            device_id_type=MESH,
        )

    for p in range(PIECES):
        core_copy(p).start()

    @pl.when(core == 1)
    def _():
        pl.semaphore_wait(barrier, 63)
        pl.semaphore_signal(all_met, inc=1, device_id=partner, device_id_type=MESH)

    @pl.when(core == 0)
    def _():
        pl.semaphore_wait(all_met, 1)

    chips = 8 // PIECES
    groups = lax.broadcasted_iota(jnp.int32, (chips, 8, 128), 2) // 32
    for p in range(PIECES):
        core_copy(p).wait_recv()
        added = mine[:, p * rows : (p + 1) * rows] + w_in[:, p * rows : (p + 1) * rows]
        added = added.reshape(2, chips, 2, 8, 256)
        for h in range(2):
            tiles = [added[g // 2, :, g % 2, :, h * 128 : h * 128 + 128] for g in range(4)]
            for q, made in enumerate(regroup(tiles, groups)):
                packed[p * chips : (p + 1) * chips, h * 4 + q] = made
        for j, k in order:
            if j // chips == p:
                pltpu.make_async_remote_copy(
                    src_ref=packed.at[j, k],
                    dst_ref=landed.at[j * 8 + k],
                    send_sem=far_send,
                    recv_sem=far_recv,
                    device_id=(row_to[j] * 2 + core, col_to[k]),
                    device_id_type=MESH,
                ).start()

    pltpu.make_async_copy(four_v, four_v, four_sem).wait()
    for c in range(2):
        f_h[c * 256 : c * 256 + 256], f_l[c * 256 : c * 256 + 256] = split(four_v[c])

    pltpu.make_async_copy(landed.at[0:63], landed.at[0:63], far_recv).wait()
    for k in range(8):
        total = landed[k]
        for j in range(1, 7):
            total = total + landed[j * 8 + k]
        total = total + (landed[56 + k] if k < 7 else packed[7, 7])
        sums[col_from[k]] = total
    group = lax.broadcasted_iota(jnp.int32, (8, 128), 1) // 32
    v = jnp.concatenate(
        [jnp.concatenate(regroup([sums[h * 4 + q] for q in range(4)], group), axis=0) for h in range(2)], axis=1
    )
    v_h, v_l = split(v)
    first = dot(jnp.concatenate([v_h, v_l], axis=0), f_h[...], NT)
    made = first[0:32] + first[32:64] + dot(v_h, f_l[...], NT)
    result = (made[0:16, 0:256] - made[16:32, 256:512], made[0:16, 256:512] + made[16:32, 0:256])
    for c in range(2):
        for b in range(8):
            out[c, b] = result[c][:, b * 32 : b * 32 + 32]

    for p in range(PIECES):
        core_copy(p).wait_send()
    pltpu.make_async_copy(landed.at[0:63], landed.at[0:63], far_send).wait()


def body(stem, branch_one, branch_two, branch_three, branch_four, relabel):
    factor = (stem.shape[3] * lax.axis_size("row")) ** (-0.5)
    any_space = pl.BlockSpec(memory_space=pltpu.HBM)
    dma = pltpu.SemaphoreType.DMA
    made = pl.pallas_call(
        functools.partial(kernel, factor),
        out_shape=pltpu.VMEM((2, 8, 16, 32), F32),
        in_specs=[any_space] * 6,
        out_specs=pl.BlockSpec(memory_space=pltpu.VMEM),
        scratch_shapes=[
            pltpu.VMEM((2, 4, 256, 256), F32),
            pltpu.VMEM((2, 8, 32, 256), F32),
            pltpu.VMEM((2, 2, 8, 16, 256), F32),
            pltpu.VMEM((2, 16, 16, 128), F32),
            pltpu.VMEM((2, 256, 256), F32),
            pltpu.VMEM((256,), jnp.int32),
            pltpu.VMEM((256, 512), BF16),
            pltpu.VMEM((512, 512), BF16),
            *[pltpu.VMEM((3, 2, 256, 256), BF16)] * 4,
            pltpu.VMEM((512, 256), BF16),
            pltpu.VMEM((512, 256), BF16),
            pltpu.VMEM((2, 128, 256), F32),
            pltpu.VMEM((2, 128, 256), F32),
            pltpu.VMEM((8, 8, 8, 128), F32),
            pltpu.VMEM((64, 8, 128), F32),
            pltpu.VMEM((8, 8, 128), F32),
            dma, dma, dma, dma, dma, dma,
            dma((PIECES,)), dma((PIECES,)), dma, dma,
            pltpu.SemaphoreType.REGULAR, pltpu.SemaphoreType.REGULAR,
        ],
        compiler_params=pltpu.CompilerParams(
            collective_id=0, has_side_effects=True, vmem_limit_bytes=40 << 20
        ),
        name="contract",
    )(
        *(
            pltpu.with_memory_space_constraint(value, pltpu.HBM)
            for value in (
                stem.reshape(2, 4, 256, 256),
                branch_one.reshape(2, 8, 32, 256),
                branch_two.reshape(2, 8, 2, 16, 256),
                branch_three.reshape(2, 16, 16, 256),
                branch_four,
                relabel,
            )
        )
    )
    return made.transpose(0, 1, 3, 2)


def solution(mesh):
    in_specs = (P(None, "row", "col", None, None, None), P(), P(), P(), P(), P())
    out_specs = P(None, None, "col", "row")
    return jax.shard_map(body, mesh=mesh, in_specs=in_specs, out_specs=out_specs, check_vma=False)
```

```python
import functools

import jax
import jax.numpy as jnp
from jax import lax
from jax.experimental import pallas as pl
from jax.experimental.pallas import tpu as pltpu
from jax.sharding import PartitionSpec as P

MESH = pl.DeviceIdType.MESH
F32, BF16 = jnp.float32, jnp.bfloat16
NT = (((1,), (1,)), ((), ()))
NN = (((1,), (0,)), ((), ()))

OFFSETS = ((1, 2), (1, 1), (1, 0), (1, 3), (0, 2), (0, 1), (0, 3), (0, 0))
PIECES = 4


def dot(lhs, rhs, dims):
    return lax.dot_general(lhs, rhs, dims, preferred_element_type=F32)


def split(value):
    high = value.astype(BF16)
    return high, (value - high.astype(F32)).astype(BF16)


def hops(j, k):
    (y_hi, x), (y_lo, z) = OFFSETS[j], OFFSETS[k]
    return min(x, 4 - x) + min(z, 4 - z) + (1 if y_lo else 2 * y_hi)


def shifted(index, offset, sign):
    high, low = index // 4, index % 4
    return ((high + 2 + sign * offset[0]) % 2) * 4 + (low + 4 + sign * offset[1]) % 4


def lanes_to(value, source, target):
    amount = (target - source) * 32 % 128
    return value if amount == 0 else pltpu.roll(value, amount, value.ndim - 1)


def regroup(tiles, lane_group):
    out = []
    for j in range(4):
        made = lanes_to(tiles[0], j, 0)
        for i in range(1, 4):
            made = jnp.where(lane_group == i, lanes_to(tiles[i], j, i), made)
        out.append(made)
    return out


def put_left(ref, real_part, imag_part, rows, width, row=0, column=0):
    for block, (re, im) in enumerate(zip(split(real_part), split(imag_part))):
        at = column + block * 2 * width
        ref[row : row + rows, at : at + width] = re
        ref[row : row + rows, at + width : at + 2 * width] = -im
        ref[row + rows : row + 2 * rows, at : at + width] = im
        ref[row + rows : row + 2 * rows, at + width : at + 2 * width] = re


def three_dots(left_high, left_low, right_high, right_low, dims):
    return dot(left_high, right_high, dims) + dot(left_low, right_high, dims) + dot(left_high, right_low, dims)


def put_three(ref, real_part, imag_part):
    for i, value in enumerate((real_part, imag_part, real_part + imag_part)):
        for part, made in enumerate(split(value)):
            ref[i, part] = made


def product(left, right, dims):
    rr, ii, ss = (three_dots(left[i, 0], left[i, 1], right[i, 0], right[i, 1], dims) for i in range(3))
    return rr - ii, ss - rr - ii


def kernel(
    factor, stem, one, two, three, four, relabel, out,
    stem_v, one_v, two_v, three_v, four_v, relabel_v,
    k_lhs, m_rhs, m_lhs, t_rhs, o_lhs, s_rhs, f_h, f_l,
    w_out, w_in, packed, landed, sums,
    stem_sem, one_sem, two_sem, three_sem, four_sem, relabel_sem,
    core_send, core_recv, far_send, far_recv, met, all_met,
):
    row, col = lax.axis_index("row"), lax.axis_index("col")
    chip, core = row // 2, row % 2
    partner = (chip * 2 + 1 - core, col)
    row_to = [shifted(chip, o, 1) for o in OFFSETS]
    col_to = [shifted(col, o, 1) for o in OFFSETS]
    col_from = [shifted(col, o, -1) for o in OFFSETS]
    order = sorted(
        ((j, k) for j in range(8) for k in range(8) if (j, k) != (7, 7)),
        key=lambda jk: -hops(*jk),
    )

    barrier = pltpu.get_barrier_semaphore()

    @pl.when(core == 1)
    def _():
        pl.semaphore_signal(barrier, inc=1, device_id=partner, device_id_type=MESH)

    pltpu.make_async_copy(relabel, relabel_v, relabel_sem).start()
    column = pl.multiple_of(row // 8 * 128, 128)
    for x in range(16):
        pltpu.make_async_copy(three.at[:, x, :, pl.ds(column, 128)], three_v.at[:, x], three_sem).start()
    @pl.when(core == 0)
    def _():
        pl.semaphore_wait(barrier, 1)
        pl.semaphore_signal(met, inc=1, device_id=partner, device_id_type=MESH)

    for j in range(8):
        for half in range(2):
            source = 1 - core if half == 0 else core
            pltpu.make_async_copy(two.at[:, row_to[j], source], two_v.at[half, :, j], two_sem).start()
    for k in range(8):
        pltpu.make_async_copy(one.at[:, col_to[k]], one_v.at[:, k], one_sem).start()
    for c in range(2):
        for f in range(0, 4, 2):
            pltpu.make_async_copy(stem.at[c, f : f + 2], stem_v.at[c, f : f + 2], stem_sem).start(priority=1)

    @pl.when(core == 1)
    def _():
        pl.semaphore_wait(met, 1)
        for j, k in order:
            pl.semaphore_signal(barrier, inc=1, device_id=(row_to[j] * 2 + 1, col_to[k]), device_id_type=MESH)

    pltpu.make_async_copy(three_v, three_v, three_sem).wait()
    lane = lax.broadcasted_iota(jnp.int32, (16, 128), 1)
    turned = (128 - row % 8 * 16) % 128
    diagonal = (
        lax.broadcasted_iota(jnp.int32, (128, 128), 0) // 16 == lax.broadcasted_iota(jnp.int32, (128, 128), 1) // 16
    )
    block = []
    for c in range(2):
        piece = three_v[c, 0]
        for x in range(1, 16):
            piece = piece + three_v[c, x]
        piece = jnp.where(lane < 16, pltpu.roll(piece * factor, turned, 1), 0.0)
        for amount in (16, 32, 64):
            piece = piece + pltpu.roll(piece, amount, 1)
        block.append(jnp.where(diagonal, jnp.concatenate([piece] * 8, axis=0), 0.0))
    put_left(k_lhs, block[0], block[1], 128, 128)

    pltpu.make_async_copy(relabel_v, relabel_v, relabel_sem).wait()
    names = jnp.broadcast_to(relabel_v[...].reshape(1, 256), (256, 256))
    pick = jnp.where(lax.broadcasted_iota(jnp.int32, (256, 256), 0) == names, 1.0, 0.0).astype(BF16)
    pltpu.make_async_copy(two_v, two_v, two_sem).wait()
    for half in range(2):
        high, low = (dot(part, pick, NT).astype(BF16) for part in split(two_v[half].reshape(256, 256)))
        for block_at, part in enumerate((high, low)):
            m_rhs[block_at * 256 : block_at * 256 + 256, half * 256 : half * 256 + 256] = part
    m_all = three_dots(k_lhs[:, 0:256], k_lhs[:, 256:512], m_rhs[0:256], m_rhs[256:512], NN)
    stacked = [
        jnp.concatenate([m_all[c * 128 : c * 128 + 128, 0:256], m_all[c * 128 : c * 128 + 128, 256:512]], axis=0)
        for c in range(2)
    ]
    put_three(m_lhs, *stacked)

    pltpu.make_async_copy(one_v, one_v, one_sem).wait()
    put_three(o_lhs, one_v[0].reshape(256, 256), one_v[1].reshape(256, 256))
    pltpu.make_async_copy(stem_v, stem_v, stem_sem).wait()
    put_three(t_rhs, *((stem_v[c, 0] + stem_v[c, 1]) + (stem_v[c, 2] + stem_v[c, 3]) for c in range(2)))
    put_three(s_rhs, *product(o_lhs, t_rhs, NN))
    pltpu.make_async_copy(four, four_v, four_sem).start()

    rows = 128 // PIECES
    w_parts = product(m_lhs, s_rhs, NT)
    for c in range(2):
        w_out[c] = w_parts[c][0:128]
    mine = jnp.stack([w_parts[c][128:256] for c in range(2)])

    def core_copy(p):
        return pltpu.make_async_remote_copy(
            src_ref=w_out.at[:, p * rows : (p + 1) * rows],
            dst_ref=w_in.at[:, p * rows : (p + 1) * rows],
            send_sem=core_send.at[p],
            recv_sem=core_recv.at[p],
            device_id=partner,
            device_id_type=MESH,
        )

    for p in range(PIECES):
        core_copy(p).start()

    @pl.when(core == 1)
    def _():
        pl.semaphore_wait(barrier, 63)
        pl.semaphore_signal(all_met, inc=1, device_id=partner, device_id_type=MESH)

    @pl.when(core == 0)
    def _():
        pl.semaphore_wait(all_met, 1)

    chips = 8 // PIECES
    groups = lax.broadcasted_iota(jnp.int32, (chips, 8, 128), 2) // 32
    for p in range(PIECES):
        core_copy(p).wait_recv()
        added = mine[:, p * rows : (p + 1) * rows] + w_in[:, p * rows : (p + 1) * rows]
        added = added.reshape(2, chips, 2, 8, 256)
        for h in range(2):
            tiles = [added[g // 2, :, g % 2, :, h * 128 : h * 128 + 128] for g in range(4)]
            for q, made in enumerate(regroup(tiles, groups)):
                packed[p * chips : (p + 1) * chips, h * 4 + q] = made
        for j, k in order:
            if j // chips == p:
                pltpu.make_async_remote_copy(
                    src_ref=packed.at[j, k],
                    dst_ref=landed.at[j * 8 + k],
                    send_sem=far_send,
                    recv_sem=far_recv,
                    device_id=(row_to[j] * 2 + core, col_to[k]),
                    device_id_type=MESH,
                ).start()

    pltpu.make_async_copy(four_v, four_v, four_sem).wait()
    for c in range(2):
        f_h[c * 256 : c * 256 + 256], f_l[c * 256 : c * 256 + 256] = split(four_v[c])

    pltpu.make_async_copy(landed.at[0:63], landed.at[0:63], far_recv).wait()
    for k in range(8):
        total = landed[k]
        for j in range(1, 7):
            total = total + landed[j * 8 + k]
        total = total + (landed[56 + k] if k < 7 else packed[7, 7])
        sums[col_from[k]] = total
    group = lax.broadcasted_iota(jnp.int32, (8, 128), 1) // 32
    v = jnp.concatenate(
        [jnp.concatenate(regroup([sums[h * 4 + q] for q in range(4)], group), axis=0) for h in range(2)], axis=1
    )
    v_h, v_l = split(v)
    first = dot(jnp.concatenate([v_h, v_l], axis=0), f_h[...], NT)
    made = first[0:32] + first[32:64] + dot(v_h, f_l[...], NT)
    result = (made[0:16, 0:256] - made[16:32, 256:512], made[0:16, 256:512] + made[16:32, 0:256])
    for c in range(2):
        for b in range(8):
            out[c, b] = result[c][:, b * 32 : b * 32 + 32]

    for p in range(PIECES):
        core_copy(p).wait_send()
    pltpu.make_async_copy(landed.at[0:63], landed.at[0:63], far_send).wait()


def body(stem, branch_one, branch_two, branch_three, branch_four, relabel):
    factor = (stem.shape[3] * lax.axis_size("row")) ** (-0.5)
    any_space = pl.BlockSpec(memory_space=pltpu.HBM)
    dma = pltpu.SemaphoreType.DMA
    made = pl.pallas_call(
        functools.partial(kernel, factor),
        out_shape=pltpu.VMEM((2, 8, 16, 32), F32),
        in_specs=[any_space] * 6,
        out_specs=pl.BlockSpec(memory_space=pltpu.VMEM),
        scratch_shapes=[
            pltpu.VMEM((2, 4, 256, 256), F32),
            pltpu.VMEM((2, 8, 32, 256), F32),
            pltpu.VMEM((2, 2, 8, 16, 256), F32),
            pltpu.VMEM((2, 16, 16, 128), F32),
            pltpu.VMEM((2, 256, 256), F32),
            pltpu.VMEM((256,), jnp.int32),
            pltpu.VMEM((256, 512), BF16),
            pltpu.VMEM((512, 512), BF16),
            *[pltpu.VMEM((3, 2, 256, 256), BF16)] * 4,
            pltpu.VMEM((512, 256), BF16),
            pltpu.VMEM((512, 256), BF16),
            pltpu.VMEM((2, 128, 256), F32),
            pltpu.VMEM((2, 128, 256), F32),
            pltpu.VMEM((8, 8, 8, 128), F32),
            pltpu.VMEM((64, 8, 128), F32),
            pltpu.VMEM((8, 8, 128), F32),
            dma, dma, dma, dma, dma, dma,
            dma((PIECES,)), dma((PIECES,)), dma, dma,
            pltpu.SemaphoreType.REGULAR, pltpu.SemaphoreType.REGULAR,
        ],
        compiler_params=pltpu.CompilerParams(
            collective_id=0, has_side_effects=True, vmem_limit_bytes=40 << 20
        ),
        name="contract",
    )(
        *(
            pltpu.with_memory_space_constraint(value, pltpu.HBM)
            for value in (
                stem.reshape(2, 4, 256, 256),
                branch_one.reshape(2, 8, 32, 256),
                branch_two.reshape(2, 8, 2, 16, 256),
                branch_three.reshape(2, 16, 16, 256),
                branch_four,
                relabel,
            )
        )
    )
    return made.transpose(0, 1, 3, 2)


def solution(mesh):
    in_specs = (P(None, "row", "col", None, None, None), P(), P(), P(), P(), P())
    out_specs = P(None, None, "col", "row")
    return jax.shard_map(body, mesh=mesh, in_specs=in_specs, out_specs=out_specs, check_vma=False)
```
